32 devices in a mesh: dp: 8 (over y, x, core), mp: 4 (over z).
Axes of the slice: x: 2, y: 2, z: 4, core: 2. Of those that a mesh axis runs over, the one named last changes fastest.
Arguments:
- image_rows: bfloat16 [100352, 384], P(('dp', 'mp')), may hold values from -5.375 to 5.375
- tall_weight: float32 [51, 5, 384], replicated, may hold values from -0.75 to 0.75
- wide_weight: float32 [5, 51, 384], replicated, may hold values from -0.75 to 0.75
- small_weight: float32 [5, 5, 384], replicated, may hold values from -0.75 to 0.75
- tall_mask: int32 [51, 5, 384], replicated, may hold values 0 or 1
- wide_mask: int32 [5, 51, 384], replicated, may hold values 0 or 1
- small_mask: int32 [5, 5, 384], replicated, may hold values 0 or 1
- bn_gain: float32 [384], replicated, may hold values from 0.3 to 3
- bn_bias: float32 [384], replicated, may hold values from -3 to 3
- ln_gain: float32 [384], replicated, may hold values from 0.5 to 1.5
- ln_bias: float32 [384], replicated, may hold values from -3 to 3
- fc1_weight: bfloat16 [384, 1536], P(None, 'mp'), may hold values from -0.3125 to 0.3125
- fc1_bias: float32 [1536], replicated, may hold values from -3 to 3
- fc2_weight: bfloat16 [1536, 384], P('mp'), may hold values from -0.21875 to 0.21875
- fc2_bias: float32 [384], replicated, may hold values from -3 to 3
- layer_scale: float32 [384], replicated, may hold values from 0.5 to 1.5
- out_grad: bfloat16 [100352, 384], P(('dp', 'mp')), may hold values from -4 to 4
Outputs:
- block_out: bfloat16 [100352, 384], P(('dp', 'mp'))
- in_grad: bfloat16 [100352, 384], P(('dp', 'mp'))
- tall_grad: float32 [51, 5, 384], replicated
- wide_grad: float32 [5, 51, 384], replicated
- small_grad: float32 [5, 5, 384], replicated
- bn_gain_grad: float32 [384], replicated
- bn_bias_grad: float32 [384], replicated
- ln_gain_grad: float32 [384], replicated
- ln_bias_grad: float32 [384], replicated
- fc1_grad: float32 [384, 1536], P(None, 'mp')
- fc1_bias_grad: float32 [1536], P('mp')
- fc2_grad: float32 [1536, 384], P('mp')
- fc2_bias_grad: float32 [384], replicated
- scale_grad: float32 [384], replicated
The draws below stay inside these ranges and needn't reach their ends.
All inputs are finite; a program needn't handle non-finite values.
Results may differ from the reference program's by a relative error of at most 0.0079.
Values may be sent and summed in bfloat16 or wider, within the bound.
No kernel may reach another device: no remote copies, remote signals or barrier semaphores. Data moves between devices by JAX's collectives and lax.ppermute only.
A program may use at most 448 MiB of HBM per device.

```python
import math
import jax
import jax.numpy as jnp
import numpy as np
from jax import lax

D = 384
FF = 1536
MAP = 14
PIX = 196
LONGK = 51
SHORTK = 5
SMALLK = 5
TOKENS = 100352


def draw_image_rows(key, part):
    key = jax.random.fold_in(key, 11)
    position = jnp.arange(TOKENS, dtype=jnp.float32) / TOKENS
    noise = jnp.clip(jax.random.normal(key, (TOKENS, D), jnp.float32), -3.0, 3.0)
    profile = 0.6 + 1.2 * position
    return jnp.clip(noise * profile[:, None], -5.375, 5.375).astype(jnp.bfloat16)


def draw_out_grad(key, part):
    key = jax.random.fold_in(key, 23)
    key_one = jax.random.fold_in(key, 0)
    position = jnp.arange(TOKENS, dtype=jnp.float32) / TOKENS
    noise = jnp.clip(jax.random.normal(key_one, (TOKENS, D), jnp.float32), -2.0, 2.0)
    profile = 0.6 + 1.2 * position
    values = noise * profile[:, None]
    return values.astype(jnp.bfloat16)


def with_ends(values, rng, low, high):
    extent = values.shape
    index_at = [jax.random.randint(jax.random.fold_in(rng, axis), (), 0, extent[axis]) for axis in range(len(extent))]
    values = values.at[tuple(index_at)].set(low)
    longest = extent.index(max(extent))
    index_at[longest] = (index_at[longest] + 1) % extent[longest]
    return values.at[tuple(index_at)].set(high)


def steps_of(rng, shape, cuts, least, top_value):
    loudness = 1.0
    for axis_at, blocks in cuts:
        heights = jax.random.uniform(jax.random.fold_in(jax.random.fold_in(rng, 6), axis_at), (blocks,), jnp.float32, least / len(cuts), top_value / len(cuts))
        loudness = loudness * jnp.repeat(jnp.exp(heights), shape[axis_at] // blocks).reshape((-1,) + (1,) * (len(shape) - 1 - axis_at))
    return loudness


def centred(own_key, extent, width, bound, pieces=(), kind=jnp.bfloat16):
    gain = steps_of(own_key, extent, pieces, -0.22, 0.18) if pieces else 1.0
    entries = jax.random.normal(own_key, extent, jnp.float32) * width * gain
    return jnp.minimum(jnp.maximum(entries, -bound), bound).astype(kind)


def setup_inputs(seed: int = 0) -> dict:
    seeds = jax.random.split(jax.random.key(seed), 18)
    image_rows = draw_image_rows(jax.random.fold_in(seeds[17], 71), 0)
    tall_weight = centred(seeds[1], (LONGK, SHORTK, D), 64 ** -0.5, 0.75, (), jnp.float32)
    wide_weight = centred(seeds[2], (SHORTK, LONGK, D), 64 ** -0.5, 0.75, (), jnp.float32)
    small_weight = centred(seeds[3], (SMALLK, SMALLK, D), 64 ** -0.5, 0.75, (), jnp.float32)
    tall_mask = with_ends((jax.random.randint(seeds[4], (LONGK, SHORTK, D), 0, 5) < 3).astype(jnp.int32), jax.random.fold_in(seeds[4], 1), 0, 1)
    wide_mask = with_ends((jax.random.randint(seeds[5], (SHORTK, LONGK, D), 0, 5) < 3).astype(jnp.int32), jax.random.fold_in(seeds[5], 1), 0, 1)
    small_mask = with_ends((jax.random.randint(seeds[6], (SMALLK, SMALLK, D), 0, 5) < 3).astype(jnp.int32), jax.random.fold_in(seeds[6], 1), 0, 1)
    bn_gain = jnp.clip(jnp.exp(jax.random.uniform(seeds[7], (D,), jnp.float32, math.log(0.3), math.log(3.0))), 0.3, 3.0)
    bn_bias = centred(seeds[8], (D,), 0.5, 3.0, (), jnp.float32)
    ln_gain = jnp.clip(jax.random.uniform(seeds[9], (D,), jnp.float32, 0.5, 1.5), 0.5, 1.5)
    ln_bias = centred(seeds[10], (D,), 0.5, 3.0, (), jnp.float32)
    fc1_weight = centred(seeds[11], (D, FF), D ** -0.5, 0.3125, ((1, 4),))
    fc1_bias = centred(seeds[12], (FF,), 0.5, 3.0, (), jnp.float32)
    fc2_weight = centred(seeds[13], (FF, D), (FF // 2) ** -0.5, 0.21875, ((0, 4),))
    fc2_bias = centred(seeds[14], (D,), 0.5, 3.0, (), jnp.float32)
    layer_scale = jnp.clip(jax.random.uniform(seeds[15], (D,), jnp.float32, 0.5, 1.5), 0.5, 1.5)
    out_grad = draw_out_grad(jax.random.fold_in(seeds[17], 71), 0)
    return dict(image_rows=image_rows, tall_weight=tall_weight, wide_weight=wide_weight, small_weight=small_weight, tall_mask=tall_mask, wide_mask=wide_mask, small_mask=small_mask, bn_gain=bn_gain, bn_bias=bn_bias, ln_gain=ln_gain, ln_bias=ln_bias, fc1_weight=fc1_weight, fc1_bias=fc1_bias, fc2_weight=fc2_weight, fc2_bias=fc2_bias, layer_scale=layer_scale, out_grad=out_grad)


@jax.custom_vjp
def low(v):
    return lax.optimization_barrier(v.astype(jnp.bfloat16)).astype(jnp.float32)

@jax.custom_vjp
def low_back(v):
    return v

def low_keep(v):
    return (low(v), None)

def low_pass(kept, grad):
    return (grad,)

def back_keep(v):
    return (v, None)

def back_low(kept, grad):
    return (low(grad),)
low.defvjp(low_keep, low_pass)
low_back.defvjp(back_keep, back_low)
norm_epsilon = 1e-05
layer_epsilon = 1e-06
highest = lax.Precision.HIGHEST

def tap_tables():
    coords = np.arange(MAP)
    row_of = np.repeat(coords, MAP)
    col_of = np.tile(coords, MAP)
    delta_rows = row_of[None, :] - row_of[:, None]
    delta_cols = col_of[None, :] - col_of[:, None]
    half_long = LONGK // 2
    half_short = SHORTK // 2
    half_small = SMALLK // 2
    sentinel = 2 * LONGK * SHORTK + SMALLK * SMALLK
    tall_valid = (np.abs(delta_rows) <= half_long) & (np.abs(delta_cols) <= half_short)
    tall_index = np.where(tall_valid, (delta_rows + half_long) * SHORTK + delta_cols + half_short, sentinel)
    wide_valid = (np.abs(delta_rows) <= half_short) & (np.abs(delta_cols) <= half_long)
    wide_index = np.where(wide_valid, LONGK * SHORTK + (delta_rows + half_short) * LONGK + delta_cols + half_long, sentinel)
    small_valid = (np.abs(delta_rows) <= half_small) & (np.abs(delta_cols) <= half_small)
    small_index = np.where(small_valid, 2 * LONGK * SHORTK + (delta_rows + half_small) * SMALLK + delta_cols + half_small, sentinel)
    return (tall_index.astype(np.int32), wide_index.astype(np.int32), small_index.astype(np.int32))

def kernel_matrix(tall_live, wide_live, small_live):
    channels = tall_live.shape[-1]
    tap_table = jnp.concatenate([tall_live.reshape(-1, channels), wide_live.reshape(-1, channels), small_live.reshape(-1, channels), jnp.zeros((1, channels), jnp.float32)], axis=0)
    tall_index, wide_index, small_index = tap_tables()
    return tap_table[tall_index] + tap_table[wide_index] + tap_table[small_index]

def forward(input_rows, tall_weight, wide_weight, small_weight, bn_gain, bn_bias, ln_gain, ln_bias, fc1_weight, fc1_bias, fc2_weight, fc2_bias, layer_scale, tall_keep, wide_keep, small_keep):
    kernel = low(kernel_matrix(tall_weight * tall_keep, wide_weight * wide_keep, small_weight * small_keep))
    images = input_rows.reshape(-1, PIX, D)
    conv = low_back(jnp.einsum('pqc,bqc->bpc', kernel, images, precision=highest)).reshape(-1, D)
    mean_conv = lax.optimization_barrier(jnp.mean(conv, axis=0))
    variance = lax.optimization_barrier(jnp.mean(conv * conv, axis=0)) - mean_conv * mean_conv
    bn_out = (conv - mean_conv) * lax.rsqrt(variance + norm_epsilon) * bn_gain + bn_bias

    def mlp_block(block_rows):
        center = block_rows - lax.optimization_barrier(jnp.mean(block_rows, axis=-1, keepdims=True))
        spread = lax.optimization_barrier(jnp.mean(center * center, axis=-1, keepdims=True))
        normed = low(center * lax.rsqrt(spread + layer_epsilon) * ln_gain + ln_bias)
        hidden = low_back(jnp.dot(normed, fc1_weight, precision=highest) + fc1_bias)
        active = low(jax.nn.gelu(hidden, approximate=True))
        project = low_back(jnp.dot(active, fc2_weight, precision=highest))
        return project + fc2_bias
    blocks = bn_out.reshape(-1, 16 * PIX, D)
    mixed = lax.map(jax.checkpoint(mlp_block), blocks).reshape(-1, D)
    return input_rows + layer_scale * mixed

def reference(image_rows, tall_weight, wide_weight, small_weight, tall_mask, wide_mask, small_mask, bn_gain, bn_bias, ln_gain, ln_bias, fc1_weight, fc1_bias, fc2_weight, fc2_bias, layer_scale, out_grad):
    tall_keep = tall_mask.astype(jnp.float32)
    wide_keep = wide_mask.astype(jnp.float32)
    small_keep = small_mask.astype(jnp.float32)

    def closed(*primals):
        return forward(*primals, tall_keep, wide_keep, small_keep)
    primals = (image_rows.astype(jnp.float32), tall_weight, wide_weight, small_weight, bn_gain, bn_bias, ln_gain, ln_bias, fc1_weight.astype(jnp.float32), fc1_bias, fc2_weight.astype(jnp.float32), fc2_bias, layer_scale)
    result_rows, pull_back = jax.vjp(closed, *primals)
    gradients = pull_back(out_grad.astype(jnp.float32))
    return (result_rows.astype(jnp.bfloat16), gradients[0].astype(jnp.bfloat16), gradients[1], gradients[2], gradients[3], gradients[4], gradients[5], gradients[6], gradients[7], gradients[8], gradients[9], gradients[10], gradients[11], gradients[12])
```

```python
import jax
import jax.numpy as jnp
import numpy as np
from jax import lax
from jax.experimental import pallas as pl
from jax.experimental.pallas import tpu as pltpu
from jax.sharding import PartitionSpec as P

MAP = 14
PIX = MAP * MAP
D = 384
LONG_LO = 25 - (MAP - 1)
SPAN = 2 * MAP - 1
BN_EPS = 1e-05
LN_EPS = 1e-06

NFREQ = 368
FROWS = 2 * NFREQ
GROUP = 4 * PIX
STEP = 2 * GROUP
WIN = 208
WIN_AT = tuple(16 * (PIX * m // 16) for m in range(4))
NTAPS = 256
REST = 245
SIDE = MAP - 3

TILE = 448
CHUNK = 256
GELU_ROWS = 64
NORM_ROWS = 112
LAST_ROWS = 112
SET = 13
FREQ_ROWS = 16
VMEM_LIMIT = 60 * 1024 * 1024
SMALL_VMEM = 4 * 1024 * 1024
FINISH_VMEM = 12 * 1024 * 1024


def tap_offsets():
    taps = [(a, b) for b in range(-2, 3) for a in range(1 - MAP, MAP)]
    for a in range(-2, 3):
        taps += [(a, b) for b in range(1 - MAP, MAP) if abs(b) > 2]
    return np.array(taps)


def bf16_pair(x):
    high = np.asarray(x, np.float32).astype(jnp.bfloat16)
    low = (np.asarray(x, np.float64) - high.astype(np.float64)).astype(np.float32).astype(jnp.bfloat16)
    return np.stack([high, low])


def transform_tables():
    freq = [
        (u, v)
        for u in range(SPAN)
        for v in range(SPAN)
        if (u, v) <= ((-u) % SPAN, (-v) % SPAN)
    ]
    freq = np.array(freq)
    count = len(freq)
    twice = np.where((freq == 0).all(axis=1), 1.0, 2.0)

    def angles(points):
        return 2 * np.pi * ((freq @ points.T) % SPAN) / SPAN

    pixels = np.stack([np.repeat(np.arange(MAP), MAP), np.tile(np.arange(MAP), MAP)], axis=1)
    theta = angles(pixels)
    forward = np.zeros((4, FROWS, WIN))
    for m in range(4):
        at = PIX * m - WIN_AT[m]
        forward[m, :count, at : at + PIX] = np.cos(theta)
        forward[m, NFREQ : NFREQ + count, at : at + PIX] = -np.sin(theta)
    inverse = np.zeros((PIX, FROWS))
    inverse[:, :count] = twice * np.cos(theta).T
    inverse[:, NFREQ : NFREQ + count] = -twice * np.sin(theta).T
    taps = tap_offsets()
    phi = angles(taps)
    from_taps = np.zeros((FROWS, NTAPS))
    from_taps[:count, : len(taps)] = np.cos(phi)
    from_taps[NFREQ : NFREQ + count, : len(taps)] = np.sin(phi)
    to_taps = np.zeros((NTAPS, FROWS))
    to_taps[: len(taps), :count] = twice * np.cos(phi).T
    to_taps[: len(taps), NFREQ : NFREQ + count] = twice * np.sin(phi).T
    as_bf16 = lambda x: x.astype(np.float32).astype(jnp.bfloat16)
    return as_bf16(forward), as_bf16(inverse), bf16_pair(from_taps), bf16_pair(to_taps)


def dot(a, b):
    return jnp.dot(a, b, preferred_element_type=jnp.float32)


def dot_t(a, b):
    return lax.dot_general(a, b, (((1,), (1,)), ((), ())), preferred_element_type=jnp.float32)


def as_float(x):
    return x.astype(jnp.float32)


def as_row(ref):
    return ref[...].reshape(1, -1)


def fold8(x):
    return jnp.sum(x.reshape(-1, 8, x.shape[-1]), axis=0)


def pair_window(ref, m):
    return jnp.concatenate(
        [ref[g * GROUP + WIN_AT[m] : g * GROUP + WIN_AT[m] + WIN, :] for g in range(2)],
        axis=1,
    )


def put_pair(ref, m, pair):
    for g in range(2):
        at = g * GROUP + PIX * m
        ref[at : at + PIX, :] = pair[:, g * D : (g + 1) * D]


def whole(a):
    return pl.BlockSpec(a.shape, lambda i, n=len(a.shape): (0,) * n)


def start_all(copies):
    for copy in copies:
        copy.start()


def wait_all(copies):
    for copy in copies:
        copy.wait()


def conv_kernel(
    image_ref, tall_ref, wide_ref, small_ref, tall_mask_ref, wide_mask_ref, small_mask_ref,
    forward_ref, inverse_ref, from_taps_ref,
    conv_ref, khat_ref, moments_ref,
    product_ref, taps_ref, sums_ref,
):
    step = pl.program_id(0)

    @pl.when(step == 0)
    def _():
        sums_ref[...] = jnp.zeros_like(sums_ref)
        taps_ref[...] = jnp.zeros_like(taps_ref)
        for b in range(5):
            column = tall_ref[b, LONG_LO : LONG_LO + SPAN] * as_float(tall_mask_ref[b, LONG_LO : LONG_LO + SPAN])
            middle = column[MAP - 3 : MAP + 2] + wide_ref[:, 23 + b, :] * as_float(wide_mask_ref[:, 23 + b, :])
            middle = middle + small_ref[:, b, :] * as_float(small_mask_ref[:, b, :])
            taps_ref[SPAN * b : SPAN * b + SPAN, :] = column
            taps_ref[SPAN * b + MAP - 3 : SPAN * b + MAP + 2, :] = middle
        for r in range(5):
            at = 5 * SPAN + 2 * SIDE * r
            for lo in (LONG_LO, 28):
                row = wide_ref[r, lo : lo + SIDE] * as_float(wide_mask_ref[r, lo : lo + SIDE])
                taps_ref[at : at + SIDE, :] = row
                at += SIDE
        taps = taps_ref[...].astype(jnp.bfloat16)
        khat = dot(from_taps_ref[0], taps) + dot(from_taps_ref[1], taps)
        khat_ref[...] = khat * np.float32(1.0 / (SPAN * SPAN))

    for k in range(2):
        images = (2 * k, 2 * k + 1)
        spectra = [dot(forward_ref[m], pair_window(image_ref, m)) for m in images]
        for r in range(0, NFREQ, FREQ_ROWS):
            re, im = slice(r, r + FREQ_ROWS), slice(NFREQ + r, NFREQ + r + FREQ_ROWS)
            real, imag = khat_ref[re, :], khat_ref[im, :]
            for m, xhat in zip(images, spectra):
                for g in range(2):
                    cols = slice(g * D, (g + 1) * D)
                    xr, xi = xhat[re, cols], xhat[im, cols]
                    product_ref[m, re, cols] = (real * xr - imag * xi).astype(jnp.bfloat16)
                    product_ref[m, im, cols] = (real * xi + imag * xr).astype(jnp.bfloat16)
        for m in images:
            put_pair(conv_ref, m, dot(inverse_ref[...], product_ref[m]))
    conv = conv_ref[...]
    sums_ref[:8, :] += fold8(conv)
    sums_ref[8:, :] += fold8(conv * conv)

    @pl.when(step == pl.num_programs(0) - 1)
    def _():
        sums = [jnp.sum(sums_ref[8 * i : 8 * i + 8, :], axis=0, keepdims=True) for i in range(2)]
        put_everywhere(moments_ref, jnp.concatenate(sums, axis=0))


def conv_forward(image_rows, weights, masks, tables):
    rows = image_rows.shape[0]
    steps = rows // STEP
    forward, inverse, from_taps, _ = tables
    khat = jax.ShapeDtypeStruct((FROWS, D), jnp.float32)
    devices = lax.axis_size("dp") * lax.axis_size("mp")
    moments = jax.ShapeDtypeStruct((devices, 2, D), jnp.float32)
    return pl.pallas_call(
        conv_kernel,
        grid=(steps,),
        in_specs=[pl.BlockSpec((STEP, D), lambda i: (i, 0))]
        + [whole(a) for a in (*weights, *masks, forward, inverse, from_taps)],
        out_specs=[
            pl.BlockSpec((STEP, D), lambda i: (i, 0)),
            whole(khat),
            whole(moments),
        ],
        out_shape=[
            jax.ShapeDtypeStruct((rows, D), jnp.float32),
            khat,
            moments,
        ],
        scratch_shapes=[
            pltpu.VMEM((4, FROWS, 2 * D), jnp.bfloat16),
            pltpu.VMEM((NTAPS, D), jnp.float32),
            pltpu.VMEM((16, D), jnp.float32),
        ],
        compiler_params=pltpu.CompilerParams(vmem_limit_bytes=VMEM_LIMIT),
        cost_estimate=pl.CostEstimate(
            flops=4 * rows * D * FROWS, bytes_accessed=rows * D * 10, transcendentals=0
        ),
        name="conv_forward",
    )(image_rows, *weights, *masks, forward, inverse, from_taps)


def put_everywhere(ref, rows):
    ref[...] = jnp.broadcast_to(rows[None], ref.shape)


def arrived(ref):
    return jnp.sum(ref[...], axis=0)


def exchange(x):
    return lax.all_to_all(x, ("dp", "mp"), split_axis=0, concat_axis=0)


def batch_norm_terms(moments_ref, total):
    moments = arrived(moments_ref)
    mean = moments[0:1, :] * np.float32(1.0 / total)
    variance = moments[1:2, :] * np.float32(1.0 / total) - mean * mean
    return mean, lax.rsqrt(variance + BN_EPS)


def split_refs(refs):
    return (*refs[:3], refs[3 : 3 + SET], refs[3 + SET : 3 + 2 * SET], *refs[3 + 2 * SET :])


def mlp_kernel(total, *refs):
    blocks = lax.axis_size("mp")
    conv_hbm, image_hbm, grad_hbm, moments_ref = refs[:4]
    vectors, refs = [as_row(ref) for ref in refs[4:11]], refs[11:]
    own, direct, other = refs[:2], refs[2 : 1 + blocks], refs[1 + blocks : 2 * blocks]
    out_hbm, dbn_hbm, gw_hbm, bn_sums_ref, vec_ref = refs[2 * blocks : 5 + 2 * blocks]
    (
        conv_all, image_all, grad_all, set_a, set_b, w1_ref, w2_ref, mixed_ref, dnormed_ref, g1_ref, g2_ref,
        gw_ref, sum_ref, tile_sems, weight_sems, gw_sems,
    ) = split_refs(refs[5 + 2 * blocks :])
    rows = conv_all.shape[0]
    tiles = rows // TILE
    hidden = blocks * D
    core, place = lax.axis_index("dp") % 2, lax.axis_index("mp")

    def rows_of_tile(t):
        return pl.ds(pl.multiple_of(t * TILE, TILE), TILE)

    def reads(t):
        at = rows_of_tile(t)
        pairs = [(conv_hbm, conv_all), (grad_hbm, grad_all), (image_hbm, image_all)]
        return [
            pltpu.make_async_copy(a.at[at], b.at[at], tile_sems.at[i, t]) for i, (a, b) in enumerate(pairs)
        ]

    def writes(t, buffers):
        at = rows_of_tile(t)
        pairs = [(buffers[3], out_hbm), (buffers[4], dbn_hbm)]
        return [
            pltpu.make_async_copy(a, b.at[at], tile_sems.at[3 + i, t]) for i, (a, b) in enumerate(pairs)
        ]

    start_all(reads(0))

    def weight_copies(first, second):
        copies = []
        for s in range(blocks):
            at = slice(s * D, (s + 1) * D)
            source = (own[0], own[1]) if s == 0 else (first[s - 1], second[s - 1])
            copies.append(pltpu.make_async_copy(source[0], w1_ref.at[:, at], weight_sems.at[0, s]))
            copies.append(pltpu.make_async_copy(source[1], w2_ref.at[at, :], weight_sems.at[1, s]))
        return copies

    @pl.when(core == 0)
    def _():
        start_all(weight_copies(direct, other))

    @pl.when(core != 0)
    def _():
        start_all(weight_copies(other, direct))

    for t in range(1, tiles):
        start_all(reads(t))

    mean, bn_inv = batch_norm_terms(moments_ref, total)
    bn_gain, bn_bias, ln_gain, ln_bias, fc2_bias, layer_scale, fc1_bias = vectors
    scale = bn_inv * bn_gain
    bias_of = [fc1_bias[:, i * D : (i + 1) * D] for i in range(blocks)]
    bias = jnp.concatenate(
        [sum(jnp.where((place ^ s) == i, bias_of[i], 0.0) for i in range(blocks)) for s in range(blocks)], axis=1
    )
    sum_ref[...] = jnp.zeros_like(sum_ref)
    g1_ref[...] = jnp.zeros_like(g1_ref)
    g2_ref[...] = jnp.zeros_like(g2_ref)
    ones_row = jnp.where(lax.broadcasted_iota(jnp.int32, (16, TILE), 0) == 0, 1.0, 0.0).astype(jnp.bfloat16)
    set_a[7][D:, :] = ones_row
    set_b[7][D:, :] = ones_row

    def wide(x):
        return jnp.broadcast_to(x, (x.shape[0], 128))

    def across(x):
        return jnp.concatenate([x] * (D // 128), axis=1)

    def fetch(t, buffers):
        wait_all(reads(t))
        at = rows_of_tile(t)
        for whole, buffer in zip((conv_all, grad_all, image_all), buffers):
            buffer[...] = whole[at, :]

    def normalize(buffers):
        conv_ref, grad_ref = buffers[:2]
        normed_ref, dproj_ref, normed_t_ref, dproj_t_ref, mu_ref, inv_ref = buffers[5:11]
        for r in range(0, TILE, NORM_ROWS):
            at = slice(r, r + NORM_ROWS)
            out = (conv_ref[at, :] - mean) * scale + bn_bias
            mu = jnp.mean(out, axis=1, keepdims=True)
            center = out - mu
            inv = lax.rsqrt(jnp.mean(center * center, axis=1, keepdims=True) + LN_EPS)
            mu_ref[at, :] = wide(mu)
            inv_ref[at, :] = wide(inv)
            normed_ref[at, :] = (center * inv * ln_gain + ln_bias).astype(jnp.bfloat16)
            grad = as_float(grad_ref[at, :])
            dproj_ref[at, :] = (grad * layer_scale).astype(jnp.bfloat16)
            sum_ref[40:48, :] += fold8(grad)
        normed_t_ref[:D, :] = jnp.transpose(normed_ref[...])
        dproj_t_ref[...] = jnp.transpose(dproj_ref[...])

    root = np.float32(np.sqrt(2.0 / np.pi))
    cubic = np.float32(0.044715 * np.sqrt(2.0 / np.pi))

    def gelu_chunk(c, buffers):
        normed_ref, dproj_ref, act_ref, dhid_ref = buffers[5], buffers[6], buffers[11], buffers[12]
        cols = slice(c * CHUNK, (c + 1) * CHUNK)
        hid_all = dot(normed_ref[...], w1_ref[:, cols])
        dact_all = dot_t(dproj_ref[...], w2_ref[cols, :])
        for r in range(0, TILE, GELU_ROWS):
            hid = hid_all[r : r + GELU_ROWS] + bias[:, cols]
            square = hid * hid
            th = jnp.tanh(hid * (root + cubic * square))
            half = 0.5 + 0.5 * th
            act = hid * half
            slope = half + act * (1.0 - th) * (root + 3 * cubic * square)
            act_ref[r : r + GELU_ROWS, cols] = act.astype(jnp.bfloat16)
            dhid_ref[r : r + GELU_ROWS, cols] = (dact_all[r : r + GELU_ROWS] * slope).astype(jnp.bfloat16)

    def finish_rows(r, buffers):
        conv_ref, grad_ref, image_ref, out_ref, dbn_ref = buffers[:5]
        mu_ref, inv_ref = buffers[9:11]
        at = slice(r, r + LAST_ROWS)
        mixed = mixed_ref[at, :] + fc2_bias
        dnormed = dnormed_ref[at, :]
        out_ref[at, :] = (as_float(image_ref[at, :]) + layer_scale * mixed).astype(jnp.bfloat16)
        conv = conv_ref[at, :] - mean
        bn_hat = conv * bn_inv
        inv = across(inv_ref[at, :])
        ln_hat = (conv * scale + bn_bias - across(mu_ref[at, :])) * inv
        d_hat = dnormed * ln_gain
        first = jnp.mean(d_hat, axis=1, keepdims=True)
        second = jnp.mean(d_hat * ln_hat, axis=1, keepdims=True)
        dbn = inv * (d_hat - first - ln_hat * second)
        dbn_ref[at, :] = dbn
        sum_ref[0:8, :] += fold8(dbn * bn_hat)
        sum_ref[8:16, :] += fold8(dbn)
        sum_ref[16:24, :] += fold8(dnormed * ln_hat)
        sum_ref[24:32, :] += fold8(dnormed)
        sum_ref[32:40, :] += fold8(as_float(grad_ref[at, :]) * mixed)

    chunks = hidden // CHUNK
    parts = TILE // LAST_ROWS

    def step(ahead, now):
        if now is not None:
            act_ref, dhid_ref = now[11:13]
            mixed_ref[...] = dot(act_ref[...], w2_ref[...])
            dnormed_ref[...] = dot_t(dhid_ref[...], w1_ref[...])
        if ahead is not None:
            normalize(ahead)
        for c in range(chunks):
            if ahead is not None:
                gelu_chunk(c, ahead)
            if now is not None:
                cols = slice(c * CHUNK, (c + 1) * CHUNK)
                g1_ref[:, cols] += dot(now[7][...], dhid_ref[:, cols])
                g2_ref[:, cols] += dot(now[8][...], act_ref[:, cols])
                for i in range(c * parts // chunks, (c + 1) * parts // chunks):
                    finish_rows(i * LAST_ROWS, now)

    def two_steps(i, _):
        fetch(2 * i + 1, set_b)

        @pl.when(i > 0)
        def _():
            wait_all(writes(2 * i - 2, set_a))

        step(set_b, set_a)
        start_all(writes(2 * i, set_a))
        fetch(2 * i + 2, set_a)

        @pl.when(i > 0)
        def _():
            wait_all(writes(2 * i - 1, set_b))

        step(set_a, set_b)
        start_all(writes(2 * i + 1, set_b))
        return 0

    fetch(0, set_a)
    wait_all(weight_copies(direct, other))
    step(set_a, None)
    lax.fori_loop(0, (tiles - 1) // 2, two_steps, 0)
    last = tiles - 1
    if tiles % 2 == 0:
        fetch(last, set_b)
        if tiles > 2:
            wait_all(writes(last - 3, set_a))
        step(set_b, set_a)
        start_all(writes(last - 1, set_a))
        if tiles > 2:
            wait_all(writes(last - 2, set_b))
        step(None, set_b)
        start_all(writes(last, set_b))
    else:
        if tiles > 1:
            wait_all(writes(last - 2, set_a))
        step(None, set_a)
        start_all(writes(last, set_a))

    chips, size = gw_ref.shape[1] // 2, gw_ref.shape[2]
    gw_copy = lambda s: pltpu.make_async_copy(gw_ref.at[s], gw_hbm.at[:, s], gw_sems.at[s])
    for s in range(blocks):
        cols = slice(s * D, (s + 1) * D)
        vec_ref[pl.ds(4 + (place ^ s), 1), :] = g1_ref[D : D + 1, cols]
        for i in range(chips):
            rows_of = slice(i * size, (i + 1) * size)
            gw_ref[s, 2 * i] = g1_ref[rows_of, cols].astype(jnp.bfloat16)
            gw_ref[s, 2 * i + 1] = g2_ref[rows_of, cols].astype(jnp.bfloat16)
        gw_copy(s).start()

    sums = [jnp.sum(sum_ref[8 * i : 8 * i + 8, :], axis=0, keepdims=True) for i in range(6)]
    put_everywhere(bn_sums_ref, jnp.concatenate(sums[:2], axis=0))
    vec_ref[0:4, :] = jnp.concatenate(sums[2:5] + [sums[5] * layer_scale], axis=0)
    for s in range(blocks):
        gw_copy(s).wait()
    first_set, second_set = (set_a, set_b) if tiles % 2 == 1 else (set_b, set_a)
    if tiles > 1:
        wait_all(writes(last - 1, second_set))
    wait_all(writes(last, first_set))


def mlp(total, conv, image_rows, out_grad, moments, vectors, own, direct, other):
    rows = conv.shape[0]
    tiles = rows // TILE
    blocks, chips = lax.axis_size("mp"), lax.axis_size("dp") // 2
    hidden = blocks * D
    vmem, hbm = pl.BlockSpec(memory_space=pltpu.VMEM), pl.BlockSpec(memory_space=pl.ANY)
    f32, bf16 = jnp.float32, jnp.bfloat16
    return pl.pallas_call(
        lambda *refs: mlp_kernel(total, *refs),
        in_specs=[hbm] * 3 + [vmem] * 8 + [hbm] * (2 * blocks),
        out_specs=[hbm] * 3 + [vmem] * 2,
        out_shape=[
            jax.ShapeDtypeStruct((rows, D), bf16),
            jax.ShapeDtypeStruct((rows, D), f32),
            jax.ShapeDtypeStruct((2 * chips, blocks, D // chips, D), bf16),
            jax.ShapeDtypeStruct((2 * chips * blocks, 2, D), f32),
            jax.ShapeDtypeStruct((4 + blocks, D), f32),
        ],
        scratch_shapes=[
            pltpu.VMEM((rows, D), f32),
            pltpu.VMEM((rows, D), bf16),
            pltpu.VMEM((rows, D), bf16),
        ]
        + [
            pltpu.VMEM((TILE, D), f32),
            pltpu.VMEM((TILE, D), bf16),
            pltpu.VMEM((TILE, D), bf16),
            pltpu.VMEM((TILE, D), bf16),
            pltpu.VMEM((TILE, D), f32),
            pltpu.VMEM((TILE, D), bf16),
            pltpu.VMEM((TILE, D), bf16),
            pltpu.VMEM((D + 16, TILE), bf16),
            pltpu.VMEM((D, TILE), bf16),
            pltpu.VMEM((TILE, 128), f32),
            pltpu.VMEM((TILE, 128), f32),
            pltpu.VMEM((TILE, hidden), bf16),
            pltpu.VMEM((TILE, hidden), bf16),
        ]
        * 2
        + [pltpu.VMEM((D, hidden), bf16), pltpu.VMEM((hidden, D), bf16)]
        + [pltpu.VMEM((TILE, D), f32)] * 2
        + [
            pltpu.VMEM((D + 16, hidden), f32),
            pltpu.VMEM((D, hidden), f32),
            pltpu.VMEM((blocks, 2 * chips, D // chips, D), bf16),
            pltpu.VMEM((48, D), f32),
            pltpu.SemaphoreType.DMA((5, tiles)),
            pltpu.SemaphoreType.DMA((2, blocks)),
            pltpu.SemaphoreType.DMA((blocks,)),
        ],
        compiler_params=pltpu.CompilerParams(vmem_limit_bytes=VMEM_LIMIT),
        cost_estimate=pl.CostEstimate(
            flops=12 * rows * D * hidden, bytes_accessed=rows * D * 20, transcendentals=rows * hidden
        ),
        name="mlp",
    )(conv, image_rows, out_grad, moments, *vectors, *own, *direct, *other)


def conv_back_kernel(
    total, dbn_ref, conv_ref, grad_ref, image_ref, khat_ref, moments_ref, bn_sums_ref, vec_ref, bn_gain_ref,
    forward_ref, inverse_ref, to_taps_ref,
    in_grad_ref, taps_ref,
    dconv_ref, image_grad_ref, product_ref, dhat_ref, all_taps_ref,
):
    step = pl.program_id(0)
    mean, bn_inv = batch_norm_terms(moments_ref, total)
    bn_sums = arrived(bn_sums_ref) * np.float32(1.0 / total)
    gain = as_row(bn_gain_ref) * bn_inv
    slope, shift = bn_sums[0:1, :], bn_sums[1:2, :]

    @pl.when(step == 0)
    def _():
        dhat_ref[...] = jnp.zeros_like(dhat_ref)

    for r in range(0, STEP, LAST_ROWS):
        at = slice(r, r + LAST_ROWS)
        bn_hat = (conv_ref[at, :] - mean) * bn_inv
        dconv = gain * (dbn_ref[at, :] - shift - bn_hat * slope)
        dconv_ref[at, :] = dconv.astype(jnp.bfloat16)
    for k in range(2):
        images = (2 * k, 2 * k + 1)
        spectra = [dot(forward_ref[m], pair_window(dconv_ref, m)) for m in images]
        image_spectra = [dot(forward_ref[m], pair_window(image_ref, m)) for m in images]
        for r in range(0, NFREQ, FREQ_ROWS):
            re, im = slice(r, r + FREQ_ROWS), slice(NFREQ + r, NFREQ + r + FREQ_ROWS)
            real, imag = khat_ref[re, :], khat_ref[im, :]
            tap_re, tap_im = [], []
            for m, ghat, xhat in zip(images, spectra, image_spectra):
                for g in range(2):
                    cols = slice(g * D, (g + 1) * D)
                    gr, gi = ghat[re, cols], ghat[im, cols]
                    product_ref[m, re, cols] = (real * gr + imag * gi).astype(jnp.bfloat16)
                    product_ref[m, im, cols] = (real * gi - imag * gr).astype(jnp.bfloat16)
                    xr, xi = xhat[re, cols], xhat[im, cols]
                    tap_re.append(xr * gr + xi * gi)
                    tap_im.append(xr * gi - xi * gr)
            dhat_ref[re, :] += tree_sum(tap_re)
            dhat_ref[im, :] += tree_sum(tap_im)
        for m in images:
            put_pair(image_grad_ref, m, dot(inverse_ref[...], product_ref[m]))
    in_grad_ref[...] = (image_grad_ref[...] + as_float(grad_ref[...])).astype(jnp.bfloat16)

    @pl.when(step == pl.num_programs(0) - 1)
    def _():
        dhat = dhat_ref[...]
        high = dhat.astype(jnp.bfloat16)
        low = (dhat - as_float(high)).astype(jnp.bfloat16)
        taps = dot(to_taps_ref[0], high) + dot(to_taps_ref[0], low) + dot(to_taps_ref[1], high)
        all_taps_ref[...] = taps * np.float32(1.0 / (SPAN * SPAN))
        all_taps_ref[REST : REST + vec_ref.shape[0], :] = vec_ref[...]
        devices, size, _ = taps_ref.shape
        for i in range(devices):
            if i * size < NTAPS:
                taps_ref[i] = all_taps_ref[i * size : (i + 1) * size, :].astype(jnp.bfloat16)
            else:
                taps_ref[i] = jnp.zeros((size, D), jnp.bfloat16)


def conv_backward(total, dbn, conv, out_grad, image_rows, khat, moments, bn_sums, vec, bn_gain, tables):
    rows = conv.shape[0]
    steps = rows // STEP
    forward, inverse, _, to_taps = tables
    devices = lax.axis_size("dp") * lax.axis_size("mp")
    f32, bf16 = jnp.float32, jnp.bfloat16
    block = pl.BlockSpec((STEP, D), lambda i: (i, 0))
    taps = jax.ShapeDtypeStruct((devices, max(8, NTAPS // devices), D), bf16)
    return pl.pallas_call(
        lambda *refs: conv_back_kernel(total, *refs),
        grid=(steps,),
        in_specs=[block] * 4
        + [whole(a) for a in (khat, moments, bn_sums, vec, bn_gain, forward, inverse, to_taps)],
        out_specs=[block, whole(taps)],
        out_shape=[jax.ShapeDtypeStruct((rows, D), bf16), taps],
        scratch_shapes=[
            pltpu.VMEM((STEP, D), bf16),
            pltpu.VMEM((STEP, D), f32),
            pltpu.VMEM((4, FROWS, 2 * D), bf16),
            pltpu.VMEM((FROWS, D), f32),
            pltpu.VMEM((NTAPS, D), f32),
        ],
        compiler_params=pltpu.CompilerParams(vmem_limit_bytes=VMEM_LIMIT),
        cost_estimate=pl.CostEstimate(
            flops=4 * rows * D * FROWS, bytes_accessed=rows * D * 18, transcendentals=0
        ),
        name="conv_backward",
    )(dbn, conv, out_grad, image_rows, khat, moments, bn_sums, vec, bn_gain, forward, inverse, to_taps)


def finish_kernel(chips, *refs):
    mine, other = refs[:chips], refs[chips : 2 * chips]
    tall_mask_ref, wide_mask_ref, small_mask_ref, bn_sums_ref = refs[2 * chips : 2 * chips + 4]
    tall_ref, wide_ref, small_ref, fc1_ref, fc2_ref = refs[2 * chips + 4 : 2 * chips + 9]
    vector_refs, taps_ref, fc2_t_ref = refs[2 * chips + 9 : -2], refs[-2], refs[-1]
    core, chip = lax.axis_index("dp") % 2, lax.axis_index("dp") // 2
    places, place = lax.axis_size("mp"), lax.axis_index("mp")
    size, count = taps_ref.shape[0] // (2 * chips * places), D // chips
    for k in range(chips):
        at = pl.ds(pl.multiple_of((chip ^ k) * count, 8), count)
        mine_rows, other_rows = as_float(mine[k][...]), as_float(other[k][...])
        for s in range(places):
            for owner, rows in ((core, mine_rows), (1 - core, other_rows)):
                device = (2 * (chip ^ k) + owner) * places + (place ^ s)
                taps_ref[pl.ds(pl.multiple_of(device * size, 8), size), :] = rows[s * size : (s + 1) * size]

        @pl.when(core == 0)
        def _():
            fc1_ref[at, :] = mine_rows[places * size :]
            fc2_t_ref[at, :] = other_rows[places * size :]

        @pl.when(core != 0)
        def _():
            fc1_ref[at, :] = other_rows[places * size :]
            fc2_t_ref[at, :] = mine_rows[places * size :]

    fc2_ref[...] = jnp.transpose(fc2_t_ref[...])
    bn_sums = arrived(bn_sums_ref)
    rows = [bn_sums[0:1], bn_sums[1:2]] + [taps_ref[REST + i : REST + i + 1, :] for i in range(4)]
    rows.append(taps_ref[pl.ds(REST + 4 + place, 1), :])
    for ref, row in zip(vector_refs, rows):
        ref[...] = row.reshape(ref.shape)
    tall_ref[...] = jnp.zeros_like(tall_ref)
    wide_ref[...] = jnp.zeros_like(wide_ref)
    for b in range(5):
        column = taps_ref[SPAN * b : SPAN * b + SPAN, :]
        middle = column[MAP - 3 : MAP + 2, :]
        tall_ref[b, LONG_LO : LONG_LO + SPAN] = column * as_float(tall_mask_ref[b, LONG_LO : LONG_LO + SPAN])
        small_ref[:, b, :] = middle * as_float(small_mask_ref[:, b, :])
        wide_ref[:, 23 + b, :] = middle * as_float(wide_mask_ref[:, 23 + b, :])
    for r in range(5):
        at = 5 * SPAN + 2 * SIDE * r
        for lo in (LONG_LO, 28):
            wide_ref[r, lo : lo + SIDE] = taps_ref[at : at + SIDE, :] * as_float(wide_mask_ref[r, lo : lo + SIDE])
            at += SIDE


def finish(mine, other, masks, bn_sums):
    chips, places = len(mine), lax.axis_size("mp")
    size = (mine[0].shape[0] - D // chips) // places
    vmem = pl.BlockSpec(memory_space=pltpu.VMEM)
    square = jax.ShapeDtypeStruct((D, D), jnp.float32)
    return pl.pallas_call(
        lambda *refs: finish_kernel(chips, *refs),
        in_specs=[vmem] * (2 * chips + 4),
        out_specs=[vmem] * 12,
        out_shape=[jax.ShapeDtypeStruct(m.shape, jnp.float32) for m in masks] + [square, square]
        + [jax.ShapeDtypeStruct((D,), jnp.float32)] * 7,
        scratch_shapes=[pltpu.VMEM((2 * chips * places * size, D), jnp.float32), pltpu.VMEM((D, D), jnp.float32)],
        compiler_params=pltpu.CompilerParams(vmem_limit_bytes=FINISH_VMEM),
        name="finish",
    )(*mine, *other, *masks, bn_sums)


def swap(x, axis, bit):
    size = lax.axis_size(axis)
    return lax.ppermute(x, axis, [(i, i ^ bit) for i in range(size)])


def swap_places(parts):
    got = [swap(x, "mp", s + 1) for s, x in reversed(list(enumerate(parts)))]
    return got[::-1]


def tree_sum(terms):
    while len(terms) > 1:
        terms = [a + b for a, b in zip(terms[::2], terms[1::2])]
    return terms[0]


def plane_steps():
    return range(2, lax.axis_size("dp"), 2)


def first_weights(fc1_weight, fc2_weight):
    mine = jnp.where(lax.axis_index("dp") % 2 == 0, fc1_weight, fc2_weight)
    powers = [1 << i for i in range(lax.axis_size("mp").bit_length() - 1)]
    return {s: swap(mine, "mp", s) for s in reversed(powers)}


def other_weights(got):
    for s in range(1, lax.axis_size("mp")):
        if s not in got:
            high = 1 << (s.bit_length() - 1)
            got[s] = swap(got[high], "mp", s ^ high)
    return [got[s] for s in range(1, lax.axis_size("mp"))]


def reduce_weight_grads(parts):
    return lax.optimization_barrier(lax.psum_scatter(parts, "dp", scatter_dimension=0, tiled=False))


def message_kernel(taps_ref, weights_ref, own_ref, *message_refs):
    taps = jnp.sum(as_float(taps_ref[...]), axis=0)
    own_ref[...] = jnp.concatenate([taps, as_float(weights_ref[0])], axis=0)
    for s, ref in enumerate(message_refs):
        ref[...] = jnp.concatenate([taps, as_float(weights_ref[s + 1])], axis=0).astype(jnp.bfloat16)


def total_kernel(own_ref, *refs):
    got, total_ref = refs[:-1], refs[-1]
    size = (total_ref.shape[0] - own_ref.shape[0]) // len(got)
    rows = [own_ref[...]] + [as_float(ref[...]) for ref in got]
    weights = tree_sum([x[size:] for x in rows])
    total_ref[...] = jnp.concatenate([x[:size] for x in rows] + [weights], axis=0).astype(jnp.bfloat16)


def reduce_rest(taps, weights):
    places, size, count = lax.axis_size("mp"), taps.shape[1], weights.shape[1]
    vmem = pl.BlockSpec(memory_space=pltpu.VMEM)
    rows = lambda n, kind: jax.ShapeDtypeStruct((n, D), kind)
    own, *messages = pl.pallas_call(
        message_kernel,
        in_specs=[vmem] * 2,
        out_specs=[vmem] * places,
        out_shape=[rows(size + count, jnp.float32)] + [rows(size + count, jnp.bfloat16)] * (places - 1),
        compiler_params=pltpu.CompilerParams(vmem_limit_bytes=SMALL_VMEM),
        name="messages",
    )(exchange(taps), weights)
    got = swap_places(messages)
    mine = pl.pallas_call(
        total_kernel,
        in_specs=[vmem] * places,
        out_specs=vmem,
        out_shape=rows(places * size + count, jnp.bfloat16),
        compiler_params=pltpu.CompilerParams(vmem_limit_bytes=SMALL_VMEM),
        name="totals",
    )(own, *got)
    mine = [mine] + [swap(mine, "dp", s) for s in plane_steps()]
    return mine, [swap(x, "dp", 1) for x in mine]


def on_device(
    image_rows, tall_weight, wide_weight, small_weight, tall_mask, wide_mask, small_mask,
    bn_gain, bn_bias, ln_gain, ln_bias, fc1_weight, fc1_bias, fc2_weight, fc2_bias, layer_scale, out_grad,
):
    rows = image_rows.shape[0]
    total = rows * lax.axis_size("dp") * lax.axis_size("mp")
    tables = tuple(jnp.asarray(t) for t in transform_tables())
    turn = lambda x: jnp.swapaxes(x, 0, 1)
    masks = (turn(tall_mask), wide_mask, small_mask)
    first = first_weights(fc1_weight, fc2_weight)

    conv, khat, moments = conv_forward(
        image_rows, (turn(tall_weight), wide_weight, small_weight), masks, tables
    )
    khat, first = lax.optimization_barrier((khat, first))
    early = {s: swap(x, "dp", 1) for s, x in first.items()}
    moments, direct, early = lax.optimization_barrier((exchange(moments), other_weights(first), early))
    other = [early[s + 1] if s + 1 in early else swap(x, "dp", 1) for s, x in enumerate(direct)]
    block_out, dbn, gw, bn_sums, vec = mlp(
        total, conv, image_rows, out_grad, moments,
        (bn_gain, bn_bias, ln_gain, ln_bias, fc2_bias, layer_scale, fc1_bias),
        (fc1_weight, fc2_weight), direct, other,
    )
    bn_sums = exchange(bn_sums)
    weights = reduce_weight_grads(gw)
    in_grad, taps = conv_backward(total, dbn, conv, out_grad, image_rows, khat, moments, bn_sums, vec, bn_gain, tables)
    mine, other = reduce_rest(taps, weights)
    tall_grad, wide_grad, small_grad, fc1_grad, fc2_grad, *vec = finish(mine, other, masks, bn_sums)
    tall_grad = turn(tall_grad)
    return (
        block_out, in_grad, tall_grad, wide_grad, small_grad, vec[0], vec[1], vec[2], vec[3],
        fc1_grad, vec[6], fc2_grad, vec[5], vec[4],
    )


def solution(mesh):
    rows, none = P(("dp", "mp"), None), P()
    return jax.shard_map(
        on_device,
        mesh=mesh,
        in_specs=(rows,) + (none,) * 10 + (P(None, "mp"), none, P("mp", None), none, none, rows),
        out_specs=(rows, rows) + (none,) * 7 + (P(None, "mp"), P("mp"), P("mp", None), none, none),
        check_vma=False,
    )
```

```python
import jax
import jax.numpy as jnp
import numpy as np
from jax import lax
from jax.experimental import pallas as pl
from jax.experimental.pallas import tpu as pltpu
from jax.sharding import PartitionSpec as P

MAP = 14
PIX = MAP * MAP
D = 384
LONG_LO = 25 - (MAP - 1)
SPAN = 2 * MAP - 1
BN_EPS = 1e-05
LN_EPS = 1e-06

NFREQ = 368
FROWS = 2 * NFREQ
GROUP = 4 * PIX
STEP = 2 * GROUP
WIN = 208
WIN_AT = tuple(16 * (PIX * m // 16) for m in range(4))
NTAPS = 256
REST = 245
SIDE = MAP - 3

TILE = 448
CHUNK = 256
GELU_ROWS = 64
NORM_ROWS = 112
LAST_ROWS = 112
SET = 13
FREQ_ROWS = 16
VMEM_LIMIT = 60 * 1024 * 1024
SMALL_VMEM = 4 * 1024 * 1024
FINISH_VMEM = 12 * 1024 * 1024


def tap_offsets():
    taps = [(a, b) for b in range(-2, 3) for a in range(1 - MAP, MAP)]
    for a in range(-2, 3):
        taps += [(a, b) for b in range(1 - MAP, MAP) if abs(b) > 2]
    return np.array(taps)


def bf16_pair(x):
    high = np.asarray(x, np.float32).astype(jnp.bfloat16)
    low = (np.asarray(x, np.float64) - high.astype(np.float64)).astype(np.float32).astype(jnp.bfloat16)
    return np.stack([high, low])


def transform_tables():
    freq = [
        (u, v)
        for u in range(SPAN)
        for v in range(SPAN)
        if (u, v) <= ((-u) % SPAN, (-v) % SPAN)
    ]
    freq = np.array(freq)
    count = len(freq)
    twice = np.where((freq == 0).all(axis=1), 1.0, 2.0)

    def angles(points):
        return 2 * np.pi * ((freq @ points.T) % SPAN) / SPAN

    pixels = np.stack([np.repeat(np.arange(MAP), MAP), np.tile(np.arange(MAP), MAP)], axis=1)
    theta = angles(pixels)
    forward = np.zeros((4, FROWS, WIN))
    for m in range(4):
        at = PIX * m - WIN_AT[m]
        forward[m, :count, at : at + PIX] = np.cos(theta)
        forward[m, NFREQ : NFREQ + count, at : at + PIX] = -np.sin(theta)
    inverse = np.zeros((PIX, FROWS))
    inverse[:, :count] = twice * np.cos(theta).T
    inverse[:, NFREQ : NFREQ + count] = -twice * np.sin(theta).T
    taps = tap_offsets()
    phi = angles(taps)
    from_taps = np.zeros((FROWS, NTAPS))
    from_taps[:count, : len(taps)] = np.cos(phi)
    from_taps[NFREQ : NFREQ + count, : len(taps)] = np.sin(phi)
    to_taps = np.zeros((NTAPS, FROWS))
    to_taps[: len(taps), :count] = twice * np.cos(phi).T
    to_taps[: len(taps), NFREQ : NFREQ + count] = twice * np.sin(phi).T
    as_bf16 = lambda x: x.astype(np.float32).astype(jnp.bfloat16)
    return as_bf16(forward), as_bf16(inverse), bf16_pair(from_taps), bf16_pair(to_taps)


def dot(a, b):
    return jnp.dot(a, b, preferred_element_type=jnp.float32)


def dot_t(a, b):
    return lax.dot_general(a, b, (((1,), (1,)), ((), ())), preferred_element_type=jnp.float32)


def as_float(x):
    return x.astype(jnp.float32)


def as_row(ref):
    return ref[...].reshape(1, -1)


def fold8(x):
    return jnp.sum(x.reshape(-1, 8, x.shape[-1]), axis=0)


def pair_window(ref, m):
    return jnp.concatenate(
        [ref[g * GROUP + WIN_AT[m] : g * GROUP + WIN_AT[m] + WIN, :] for g in range(2)],
        axis=1,
    )


def put_pair(ref, m, pair):
    for g in range(2):
        at = g * GROUP + PIX * m
        ref[at : at + PIX, :] = pair[:, g * D : (g + 1) * D]


def whole(a):
    return pl.BlockSpec(a.shape, lambda i, n=len(a.shape): (0,) * n)


def start_all(copies):
    for copy in copies:
        copy.start()


def wait_all(copies):
    for copy in copies:
        copy.wait()


def conv_kernel(
    image_ref, tall_ref, wide_ref, small_ref, tall_mask_ref, wide_mask_ref, small_mask_ref,
    forward_ref, inverse_ref, from_taps_ref,
    conv_ref, khat_ref, moments_ref,
    product_ref, taps_ref, sums_ref,
):
    step = pl.program_id(0)

    @pl.when(step == 0)
    def _():
        sums_ref[...] = jnp.zeros_like(sums_ref)
        taps_ref[...] = jnp.zeros_like(taps_ref)
        for b in range(5):
            column = tall_ref[b, LONG_LO : LONG_LO + SPAN] * as_float(tall_mask_ref[b, LONG_LO : LONG_LO + SPAN])
            middle = column[MAP - 3 : MAP + 2] + wide_ref[:, 23 + b, :] * as_float(wide_mask_ref[:, 23 + b, :])
            middle = middle + small_ref[:, b, :] * as_float(small_mask_ref[:, b, :])
            taps_ref[SPAN * b : SPAN * b + SPAN, :] = column
            taps_ref[SPAN * b + MAP - 3 : SPAN * b + MAP + 2, :] = middle
        for r in range(5):
            at = 5 * SPAN + 2 * SIDE * r
            for lo in (LONG_LO, 28):
                row = wide_ref[r, lo : lo + SIDE] * as_float(wide_mask_ref[r, lo : lo + SIDE])
                taps_ref[at : at + SIDE, :] = row
                at += SIDE
        taps = taps_ref[...].astype(jnp.bfloat16)
        khat = dot(from_taps_ref[0], taps) + dot(from_taps_ref[1], taps)
        khat_ref[...] = khat * np.float32(1.0 / (SPAN * SPAN))

    for k in range(2):
        images = (2 * k, 2 * k + 1)
        spectra = [dot(forward_ref[m], pair_window(image_ref, m)) for m in images]
        for r in range(0, NFREQ, FREQ_ROWS):
            re, im = slice(r, r + FREQ_ROWS), slice(NFREQ + r, NFREQ + r + FREQ_ROWS)
            real, imag = khat_ref[re, :], khat_ref[im, :]
            for m, xhat in zip(images, spectra):
                for g in range(2):
                    cols = slice(g * D, (g + 1) * D)
                    xr, xi = xhat[re, cols], xhat[im, cols]
                    product_ref[m, re, cols] = (real * xr - imag * xi).astype(jnp.bfloat16)
                    product_ref[m, im, cols] = (real * xi + imag * xr).astype(jnp.bfloat16)
        for m in images:
            put_pair(conv_ref, m, dot(inverse_ref[...], product_ref[m]))
    conv = conv_ref[...]
    sums_ref[:8, :] += fold8(conv)
    sums_ref[8:, :] += fold8(conv * conv)

    @pl.when(step == pl.num_programs(0) - 1)
    def _():
        sums = [jnp.sum(sums_ref[8 * i : 8 * i + 8, :], axis=0, keepdims=True) for i in range(2)]
        put_everywhere(moments_ref, jnp.concatenate(sums, axis=0))


def conv_forward(image_rows, weights, masks, tables):
    rows = image_rows.shape[0]
    steps = rows // STEP
    forward, inverse, from_taps, _ = tables
    khat = jax.ShapeDtypeStruct((FROWS, D), jnp.float32)
    devices = lax.axis_size("dp") * lax.axis_size("mp")
    moments = jax.ShapeDtypeStruct((devices, 2, D), jnp.float32)
    return pl.pallas_call(
        conv_kernel,
        grid=(steps,),
        in_specs=[pl.BlockSpec((STEP, D), lambda i: (i, 0))]
        + [whole(a) for a in (*weights, *masks, forward, inverse, from_taps)],
        out_specs=[
            pl.BlockSpec((STEP, D), lambda i: (i, 0)),
            whole(khat),
            whole(moments),
        ],
        out_shape=[
            jax.ShapeDtypeStruct((rows, D), jnp.float32),
            khat,
            moments,
        ],
        scratch_shapes=[
            pltpu.VMEM((4, FROWS, 2 * D), jnp.bfloat16),
            pltpu.VMEM((NTAPS, D), jnp.float32),
            pltpu.VMEM((16, D), jnp.float32),
        ],
        compiler_params=pltpu.CompilerParams(vmem_limit_bytes=VMEM_LIMIT),
        cost_estimate=pl.CostEstimate(
            flops=4 * rows * D * FROWS, bytes_accessed=rows * D * 10, transcendentals=0
        ),
        name="conv_forward",
    )(image_rows, *weights, *masks, forward, inverse, from_taps)


def put_everywhere(ref, rows):
    ref[...] = jnp.broadcast_to(rows[None], ref.shape)


def arrived(ref):
    return jnp.sum(ref[...], axis=0)


def exchange(x):
    return lax.all_to_all(x, ("dp", "mp"), split_axis=0, concat_axis=0)


def batch_norm_terms(moments_ref, total):
    moments = arrived(moments_ref)
    mean = moments[0:1, :] * np.float32(1.0 / total)
    variance = moments[1:2, :] * np.float32(1.0 / total) - mean * mean
    return mean, lax.rsqrt(variance + BN_EPS)


def split_refs(refs):
    return (*refs[:3], refs[3 : 3 + SET], refs[3 + SET : 3 + 2 * SET], *refs[3 + 2 * SET :])


def mlp_kernel(total, *refs):
    blocks = lax.axis_size("mp")
    conv_hbm, image_hbm, grad_hbm, moments_ref = refs[:4]
    vectors, refs = [as_row(ref) for ref in refs[4:11]], refs[11:]
    own, direct, other = refs[:2], refs[2 : 1 + blocks], refs[1 + blocks : 2 * blocks]
    out_hbm, dbn_hbm, gw_hbm, bn_sums_ref, vec_ref = refs[2 * blocks : 5 + 2 * blocks]
    (
        conv_all, image_all, grad_all, set_a, set_b, w1_ref, w2_ref, mixed_ref, dnormed_ref, g1_ref, g2_ref,
        gw_ref, sum_ref, tile_sems, weight_sems, gw_sems,
    ) = split_refs(refs[5 + 2 * blocks :])
    rows = conv_all.shape[0]
    tiles = rows // TILE
    hidden = blocks * D
    core, place = lax.axis_index("dp") % 2, lax.axis_index("mp")

    def rows_of_tile(t):
        return pl.ds(pl.multiple_of(t * TILE, TILE), TILE)

    def reads(t):
        at = rows_of_tile(t)
        pairs = [(conv_hbm, conv_all), (grad_hbm, grad_all), (image_hbm, image_all)]
        return [
            pltpu.make_async_copy(a.at[at], b.at[at], tile_sems.at[i, t]) for i, (a, b) in enumerate(pairs)
        ]

    def writes(t, buffers):
        at = rows_of_tile(t)
        pairs = [(buffers[3], out_hbm), (buffers[4], dbn_hbm)]
        return [
            pltpu.make_async_copy(a, b.at[at], tile_sems.at[3 + i, t]) for i, (a, b) in enumerate(pairs)
        ]

    start_all(reads(0))

    def weight_copies(first, second):
        copies = []
        for s in range(blocks):
            at = slice(s * D, (s + 1) * D)
            source = (own[0], own[1]) if s == 0 else (first[s - 1], second[s - 1])
            copies.append(pltpu.make_async_copy(source[0], w1_ref.at[:, at], weight_sems.at[0, s]))
            copies.append(pltpu.make_async_copy(source[1], w2_ref.at[at, :], weight_sems.at[1, s]))
        return copies

    @pl.when(core == 0)
    def _():
        start_all(weight_copies(direct, other))

    @pl.when(core != 0)
    def _():
        start_all(weight_copies(other, direct))

    for t in range(1, tiles):
        start_all(reads(t))

    mean, bn_inv = batch_norm_terms(moments_ref, total)
    bn_gain, bn_bias, ln_gain, ln_bias, fc2_bias, layer_scale, fc1_bias = vectors
    scale = bn_inv * bn_gain
    bias_of = [fc1_bias[:, i * D : (i + 1) * D] for i in range(blocks)]
    bias = jnp.concatenate(
        [sum(jnp.where((place ^ s) == i, bias_of[i], 0.0) for i in range(blocks)) for s in range(blocks)], axis=1
    )
    sum_ref[...] = jnp.zeros_like(sum_ref)
    g1_ref[...] = jnp.zeros_like(g1_ref)
    g2_ref[...] = jnp.zeros_like(g2_ref)
    ones_row = jnp.where(lax.broadcasted_iota(jnp.int32, (16, TILE), 0) == 0, 1.0, 0.0).astype(jnp.bfloat16)
    set_a[7][D:, :] = ones_row
    set_b[7][D:, :] = ones_row

    def wide(x):
        return jnp.broadcast_to(x, (x.shape[0], 128))

    def across(x):
        return jnp.concatenate([x] * (D // 128), axis=1)

    def fetch(t, buffers):
        wait_all(reads(t))
        at = rows_of_tile(t)
        for whole, buffer in zip((conv_all, grad_all, image_all), buffers):
            buffer[...] = whole[at, :]

    def normalize(buffers):
        conv_ref, grad_ref = buffers[:2]
        normed_ref, dproj_ref, normed_t_ref, dproj_t_ref, mu_ref, inv_ref = buffers[5:11]
        for r in range(0, TILE, NORM_ROWS):
            at = slice(r, r + NORM_ROWS)
            out = (conv_ref[at, :] - mean) * scale + bn_bias
            mu = jnp.mean(out, axis=1, keepdims=True)
            center = out - mu
            inv = lax.rsqrt(jnp.mean(center * center, axis=1, keepdims=True) + LN_EPS)
            mu_ref[at, :] = wide(mu)
            inv_ref[at, :] = wide(inv)
            normed_ref[at, :] = (center * inv * ln_gain + ln_bias).astype(jnp.bfloat16)
            grad = as_float(grad_ref[at, :])
            dproj_ref[at, :] = (grad * layer_scale).astype(jnp.bfloat16)
            sum_ref[40:48, :] += fold8(grad)
        normed_t_ref[:D, :] = jnp.transpose(normed_ref[...])
        dproj_t_ref[...] = jnp.transpose(dproj_ref[...])

    root = np.float32(np.sqrt(2.0 / np.pi))
    cubic = np.float32(0.044715 * np.sqrt(2.0 / np.pi))

    def gelu_chunk(c, buffers):
        normed_ref, dproj_ref, act_ref, dhid_ref = buffers[5], buffers[6], buffers[11], buffers[12]
        cols = slice(c * CHUNK, (c + 1) * CHUNK)
        hid_all = dot(normed_ref[...], w1_ref[:, cols])
        dact_all = dot_t(dproj_ref[...], w2_ref[cols, :])
        for r in range(0, TILE, GELU_ROWS):
            hid = hid_all[r : r + GELU_ROWS] + bias[:, cols]
            square = hid * hid
            th = jnp.tanh(hid * (root + cubic * square))
            half = 0.5 + 0.5 * th
            act = hid * half
            slope = half + act * (1.0 - th) * (root + 3 * cubic * square)
            act_ref[r : r + GELU_ROWS, cols] = act.astype(jnp.bfloat16)
            dhid_ref[r : r + GELU_ROWS, cols] = (dact_all[r : r + GELU_ROWS] * slope).astype(jnp.bfloat16)

    def finish_rows(r, buffers):
        conv_ref, grad_ref, image_ref, out_ref, dbn_ref = buffers[:5]
        mu_ref, inv_ref = buffers[9:11]
        at = slice(r, r + LAST_ROWS)
        mixed = mixed_ref[at, :] + fc2_bias
        dnormed = dnormed_ref[at, :]
        out_ref[at, :] = (as_float(image_ref[at, :]) + layer_scale * mixed).astype(jnp.bfloat16)
        conv = conv_ref[at, :] - mean
        bn_hat = conv * bn_inv
        inv = across(inv_ref[at, :])
        ln_hat = (conv * scale + bn_bias - across(mu_ref[at, :])) * inv
        d_hat = dnormed * ln_gain
        first = jnp.mean(d_hat, axis=1, keepdims=True)
        second = jnp.mean(d_hat * ln_hat, axis=1, keepdims=True)
        dbn = inv * (d_hat - first - ln_hat * second)
        dbn_ref[at, :] = dbn
        sum_ref[0:8, :] += fold8(dbn * bn_hat)
        sum_ref[8:16, :] += fold8(dbn)
        sum_ref[16:24, :] += fold8(dnormed * ln_hat)
        sum_ref[24:32, :] += fold8(dnormed)
        sum_ref[32:40, :] += fold8(as_float(grad_ref[at, :]) * mixed)

    chunks = hidden // CHUNK
    parts = TILE // LAST_ROWS

    def step(ahead, now):
        if now is not None:
            act_ref, dhid_ref = now[11:13]
            mixed_ref[...] = dot(act_ref[...], w2_ref[...])
            dnormed_ref[...] = dot_t(dhid_ref[...], w1_ref[...])
        if ahead is not None:
            normalize(ahead)
        for c in range(chunks):
            if ahead is not None:
                gelu_chunk(c, ahead)
            if now is not None:
                cols = slice(c * CHUNK, (c + 1) * CHUNK)
                g1_ref[:, cols] += dot(now[7][...], dhid_ref[:, cols])
                g2_ref[:, cols] += dot(now[8][...], act_ref[:, cols])
                for i in range(c * parts // chunks, (c + 1) * parts // chunks):
                    finish_rows(i * LAST_ROWS, now)

    def two_steps(i, _):
        fetch(2 * i + 1, set_b)

        @pl.when(i > 0)
        def _():
            wait_all(writes(2 * i - 2, set_a))

        step(set_b, set_a)
        start_all(writes(2 * i, set_a))
        fetch(2 * i + 2, set_a)

        @pl.when(i > 0)
        def _():
            wait_all(writes(2 * i - 1, set_b))

        step(set_a, set_b)
        start_all(writes(2 * i + 1, set_b))
        return 0

    fetch(0, set_a)
    wait_all(weight_copies(direct, other))
    step(set_a, None)
    lax.fori_loop(0, (tiles - 1) // 2, two_steps, 0)
    last = tiles - 1
    if tiles % 2 == 0:
        fetch(last, set_b)
        if tiles > 2:
            wait_all(writes(last - 3, set_a))
        step(set_b, set_a)
        start_all(writes(last - 1, set_a))
        if tiles > 2:
            wait_all(writes(last - 2, set_b))
        step(None, set_b)
        start_all(writes(last, set_b))
    else:
        if tiles > 1:
            wait_all(writes(last - 2, set_a))
        step(None, set_a)
        start_all(writes(last, set_a))

    chips, size = gw_ref.shape[1] // 2, gw_ref.shape[2]
    ring = plane_ring(2 * chips)
    gw_copy = lambda s: pltpu.make_async_copy(gw_ref.at[s], gw_hbm.at[:, s], gw_sems.at[s])
    for s in range(blocks):
        cols = slice(s * D, (s + 1) * D)
        vec_ref[pl.ds(4 + (place ^ s), 1), :] = g1_ref[D : D + 1, cols]
        for i in range(chips):
            rows_of = slice(i * size, (i + 1) * size)
            gw_ref[s, ring.index(2 * i)] = g1_ref[rows_of, cols].astype(jnp.bfloat16)
            gw_ref[s, ring.index(2 * i + 1)] = g2_ref[rows_of, cols].astype(jnp.bfloat16)
        gw_copy(s).start()

    sums = [jnp.sum(sum_ref[8 * i : 8 * i + 8, :], axis=0, keepdims=True) for i in range(6)]
    put_everywhere(bn_sums_ref, jnp.concatenate(sums[:2], axis=0))
    vec_ref[0:4, :] = jnp.concatenate(sums[2:5] + [sums[5] * layer_scale], axis=0)
    for s in range(blocks):
        gw_copy(s).wait()
    first_set, second_set = (set_a, set_b) if tiles % 2 == 1 else (set_b, set_a)
    if tiles > 1:
        wait_all(writes(last - 1, second_set))
    wait_all(writes(last, first_set))


def mlp(total, conv, image_rows, out_grad, moments, vectors, own, direct, other):
    rows = conv.shape[0]
    tiles = rows // TILE
    blocks, chips = lax.axis_size("mp"), lax.axis_size("dp") // 2
    hidden = blocks * D
    vmem, hbm = pl.BlockSpec(memory_space=pltpu.VMEM), pl.BlockSpec(memory_space=pl.ANY)
    f32, bf16 = jnp.float32, jnp.bfloat16
    return pl.pallas_call(
        lambda *refs: mlp_kernel(total, *refs),
        in_specs=[hbm] * 3 + [vmem] * 8 + [hbm] * (2 * blocks),
        out_specs=[hbm] * 3 + [vmem] * 2,
        out_shape=[
            jax.ShapeDtypeStruct((rows, D), bf16),
            jax.ShapeDtypeStruct((rows, D), f32),
            jax.ShapeDtypeStruct((2 * chips, blocks, D // chips, D), bf16),
            jax.ShapeDtypeStruct((2 * chips * blocks, 2, D), f32),
            jax.ShapeDtypeStruct((4 + blocks, D), f32),
        ],
        scratch_shapes=[
            pltpu.VMEM((rows, D), f32),
            pltpu.VMEM((rows, D), bf16),
            pltpu.VMEM((rows, D), bf16),
        ]
        + [
            pltpu.VMEM((TILE, D), f32),
            pltpu.VMEM((TILE, D), bf16),
            pltpu.VMEM((TILE, D), bf16),
            pltpu.VMEM((TILE, D), bf16),
            pltpu.VMEM((TILE, D), f32),
            pltpu.VMEM((TILE, D), bf16),
            pltpu.VMEM((TILE, D), bf16),
            pltpu.VMEM((D + 16, TILE), bf16),
            pltpu.VMEM((D, TILE), bf16),
            pltpu.VMEM((TILE, 128), f32),
            pltpu.VMEM((TILE, 128), f32),
            pltpu.VMEM((TILE, hidden), bf16),
            pltpu.VMEM((TILE, hidden), bf16),
        ]
        * 2
        + [pltpu.VMEM((D, hidden), bf16), pltpu.VMEM((hidden, D), bf16)]
        + [pltpu.VMEM((TILE, D), f32)] * 2
        + [
            pltpu.VMEM((D + 16, hidden), f32),
            pltpu.VMEM((D, hidden), f32),
            pltpu.VMEM((blocks, 2 * chips, D // chips, D), bf16),
            pltpu.VMEM((48, D), f32),
            pltpu.SemaphoreType.DMA((5, tiles)),
            pltpu.SemaphoreType.DMA((2, blocks)),
            pltpu.SemaphoreType.DMA((blocks,)),
        ],
        compiler_params=pltpu.CompilerParams(vmem_limit_bytes=VMEM_LIMIT),
        cost_estimate=pl.CostEstimate(
            flops=12 * rows * D * hidden, bytes_accessed=rows * D * 20, transcendentals=rows * hidden
        ),
        name="mlp",
    )(conv, image_rows, out_grad, moments, *vectors, *own, *direct, *other)


def spectra_kernel(
    total, dbn_ref, conv_ref, image_ref, khat_ref, moments_ref, bn_sums_ref, vec_ref, bn_gain_ref,
    forward_ref, to_taps_ref,
    product_ref, taps_ref,
    dconv_ref, dhat_ref, all_taps_ref,
):
    step = pl.program_id(0)
    mean, bn_inv = batch_norm_terms(moments_ref, total)
    bn_sums = arrived(bn_sums_ref) * np.float32(1.0 / total)
    gain = as_row(bn_gain_ref) * bn_inv
    slope, shift = bn_sums[0:1, :], bn_sums[1:2, :]

    @pl.when(step == 0)
    def _():
        dhat_ref[...] = jnp.zeros_like(dhat_ref)

    for r in range(0, STEP, LAST_ROWS):
        at = slice(r, r + LAST_ROWS)
        bn_hat = (conv_ref[at, :] - mean) * bn_inv
        dconv = gain * (dbn_ref[at, :] - shift - bn_hat * slope)
        dconv_ref[at, :] = dconv.astype(jnp.bfloat16)
    for k in range(2):
        images = (2 * k, 2 * k + 1)
        spectra = [dot(forward_ref[m], pair_window(dconv_ref, m)) for m in images]
        image_spectra = [dot(forward_ref[m], pair_window(image_ref, m)) for m in images]
        for r in range(0, NFREQ, FREQ_ROWS):
            re, im = slice(r, r + FREQ_ROWS), slice(NFREQ + r, NFREQ + r + FREQ_ROWS)
            real, imag = khat_ref[re, :], khat_ref[im, :]
            tap_re, tap_im = [], []
            for m, ghat, xhat in zip(images, spectra, image_spectra):
                for g in range(2):
                    cols = slice(g * D, (g + 1) * D)
                    gr, gi = ghat[re, cols], ghat[im, cols]
                    product_ref[m, re, cols] = (real * gr + imag * gi).astype(jnp.bfloat16)
                    product_ref[m, im, cols] = (real * gi - imag * gr).astype(jnp.bfloat16)
                    xr, xi = xhat[re, cols], xhat[im, cols]
                    tap_re.append(xr * gr + xi * gi)
                    tap_im.append(xr * gi - xi * gr)
            dhat_ref[re, :] += tree_sum(tap_re)
            dhat_ref[im, :] += tree_sum(tap_im)

    @pl.when(step == pl.num_programs(0) - 1)
    def _():
        dhat = dhat_ref[...]
        high = dhat.astype(jnp.bfloat16)
        low = (dhat - as_float(high)).astype(jnp.bfloat16)
        taps = dot(to_taps_ref[0], high) + dot(to_taps_ref[0], low) + dot(to_taps_ref[1], high)
        all_taps_ref[...] = taps * np.float32(1.0 / (SPAN * SPAN))
        all_taps_ref[REST : REST + vec_ref.shape[0], :] = vec_ref[...]
        devices, size, _ = taps_ref.shape
        for i in range(devices):
            if i * size < NTAPS:
                taps_ref[i] = all_taps_ref[i * size : (i + 1) * size, :].astype(jnp.bfloat16)
            else:
                taps_ref[i] = jnp.zeros((size, D), jnp.bfloat16)


def gradient_spectra(total, dbn, conv, image_rows, khat, moments, bn_sums, vec, bn_gain, tables):
    rows = conv.shape[0]
    steps = rows // STEP
    forward, _, _, to_taps = tables
    devices = lax.axis_size("dp") * lax.axis_size("mp")
    f32, bf16 = jnp.float32, jnp.bfloat16
    block = pl.BlockSpec((STEP, D), lambda i: (i, 0))
    spectra = pl.BlockSpec((4, FROWS, 2 * D), lambda i: (i, 0, 0))
    taps = jax.ShapeDtypeStruct((devices, max(8, NTAPS // devices), D), bf16)
    return pl.pallas_call(
        lambda *refs: spectra_kernel(total, *refs),
        grid=(steps,),
        in_specs=[block] * 3
        + [whole(a) for a in (khat, moments, bn_sums, vec, bn_gain, forward, to_taps)],
        out_specs=[spectra, whole(taps)],
        out_shape=[jax.ShapeDtypeStruct((4 * steps, FROWS, 2 * D), bf16), taps],
        scratch_shapes=[
            pltpu.VMEM((STEP, D), bf16),
            pltpu.VMEM((FROWS, D), f32),
            pltpu.VMEM((NTAPS, D), f32),
        ],
        compiler_params=pltpu.CompilerParams(vmem_limit_bytes=VMEM_LIMIT),
        cost_estimate=pl.CostEstimate(
            flops=2 * rows * D * FROWS, bytes_accessed=rows * D * 26, transcendentals=0
        ),
        name="gradient_spectra",
    )(dbn, conv, image_rows, khat, moments, bn_sums, vec, bn_gain, forward, to_taps)


def inverse_kernel(product_ref, grad_ref, inverse_ref, in_grad_ref, image_grad_ref):
    for m in range(4):
        put_pair(image_grad_ref, m, dot(inverse_ref[...], product_ref[m]))
    in_grad_ref[...] = (image_grad_ref[...] + as_float(grad_ref[...])).astype(jnp.bfloat16)


def image_gradient(product, out_grad, tables):
    rows = out_grad.shape[0]
    inverse = tables[1]
    block = pl.BlockSpec((STEP, D), lambda i: (i, 0))
    return pl.pallas_call(
        inverse_kernel,
        grid=(rows // STEP,),
        in_specs=[pl.BlockSpec((4, FROWS, 2 * D), lambda i: (i, 0, 0)), block, whole(inverse)],
        out_specs=block,
        out_shape=jax.ShapeDtypeStruct((rows, D), jnp.bfloat16),
        scratch_shapes=[pltpu.VMEM((STEP, D), jnp.float32)],
        compiler_params=pltpu.CompilerParams(vmem_limit_bytes=VMEM_LIMIT),
        cost_estimate=pl.CostEstimate(
            flops=2 * rows * D * FROWS, bytes_accessed=rows * D * 10, transcendentals=0
        ),
        name="image_gradient",
    )(product, out_grad, inverse)


def finish_kernel(chips, *refs):
    mine, other = refs[:chips], refs[chips : 2 * chips]
    tall_mask_ref, wide_mask_ref, small_mask_ref, bn_sums_ref = refs[2 * chips : 2 * chips + 4]
    tall_ref, wide_ref, small_ref, fc1_ref, fc2_ref = refs[2 * chips + 4 : 2 * chips + 9]
    vector_refs, taps_ref, fc2_t_ref = refs[2 * chips + 9 : -2], refs[-2], refs[-1]
    core, chip = lax.axis_index("dp") % 2, lax.axis_index("dp") // 2
    places, place = lax.axis_size("mp"), lax.axis_index("mp")
    size, count = taps_ref.shape[0] // (2 * chips * places), D // chips
    for k in range(chips):
        at = pl.ds(pl.multiple_of((chip ^ k) * count, 8), count)
        mine_rows, other_rows = as_float(mine[k][...]), as_float(other[k][...])
        for s in range(places):
            for owner, rows in ((core, mine_rows), (1 - core, other_rows)):
                device = (2 * (chip ^ k) + owner) * places + (place ^ s)
                taps_ref[pl.ds(pl.multiple_of(device * size, 8), size), :] = rows[s * size : (s + 1) * size]

        @pl.when(core == 0)
        def _():
            fc1_ref[at, :] = mine_rows[places * size :]
            fc2_t_ref[at, :] = other_rows[places * size :]

        @pl.when(core != 0)
        def _():
            fc1_ref[at, :] = other_rows[places * size :]
            fc2_t_ref[at, :] = mine_rows[places * size :]

    fc2_ref[...] = jnp.transpose(fc2_t_ref[...])
    bn_sums = arrived(bn_sums_ref)
    rows = [bn_sums[0:1], bn_sums[1:2]] + [taps_ref[REST + i : REST + i + 1, :] for i in range(4)]
    rows.append(taps_ref[pl.ds(REST + 4 + place, 1), :])
    for ref, row in zip(vector_refs, rows):
        ref[...] = row.reshape(ref.shape)
    tall_ref[...] = jnp.zeros_like(tall_ref)
    wide_ref[...] = jnp.zeros_like(wide_ref)
    for b in range(5):
        column = taps_ref[SPAN * b : SPAN * b + SPAN, :]
        middle = column[MAP - 3 : MAP + 2, :]
        tall_ref[b, LONG_LO : LONG_LO + SPAN] = column * as_float(tall_mask_ref[b, LONG_LO : LONG_LO + SPAN])
        small_ref[:, b, :] = middle * as_float(small_mask_ref[:, b, :])
        wide_ref[:, 23 + b, :] = middle * as_float(wide_mask_ref[:, 23 + b, :])
    for r in range(5):
        at = 5 * SPAN + 2 * SIDE * r
        for lo in (LONG_LO, 28):
            wide_ref[r, lo : lo + SIDE] = taps_ref[at : at + SIDE, :] * as_float(wide_mask_ref[r, lo : lo + SIDE])
            at += SIDE


def finish(mine, other, masks, bn_sums):
    chips, places = len(mine), lax.axis_size("mp")
    size = (mine[0].shape[0] - D // chips) // places
    vmem = pl.BlockSpec(memory_space=pltpu.VMEM)
    square = jax.ShapeDtypeStruct((D, D), jnp.float32)
    return pl.pallas_call(
        lambda *refs: finish_kernel(chips, *refs),
        in_specs=[vmem] * (2 * chips + 4),
        out_specs=[vmem] * 12,
        out_shape=[jax.ShapeDtypeStruct(m.shape, jnp.float32) for m in masks] + [square, square]
        + [jax.ShapeDtypeStruct((D,), jnp.float32)] * 7,
        scratch_shapes=[pltpu.VMEM((2 * chips * places * size, D), jnp.float32), pltpu.VMEM((D, D), jnp.float32)],
        compiler_params=pltpu.CompilerParams(vmem_limit_bytes=FINISH_VMEM),
        name="finish",
    )(*mine, *other, *masks, bn_sums)


def swap(x, axis, bit):
    size = lax.axis_size(axis)
    return lax.ppermute(x, axis, [(i, i ^ bit) for i in range(size)])


def swap_places(parts):
    got = [swap(x, "mp", s + 1) for s, x in reversed(list(enumerate(parts)))]
    return got[::-1]


def tree_sum(terms):
    while len(terms) > 1:
        terms = [a + b for a, b in zip(terms[::2], terms[1::2])]
    return terms[0]


def plane_steps():
    return range(2, lax.axis_size("dp"), 2)


def first_weights(fc1_weight, fc2_weight):
    mine = jnp.where(lax.axis_index("dp") % 2 == 0, fc1_weight, fc2_weight)
    powers = [1 << i for i in range(lax.axis_size("mp").bit_length() - 1)]
    return {s: swap(mine, "mp", s) for s in reversed(powers)}


def other_weights(got):
    for s in range(1, lax.axis_size("mp")):
        if s not in got:
            high = 1 << (s.bit_length() - 1)
            got[s] = swap(got[high], "mp", s ^ high)
    return [got[s] for s in range(1, lax.axis_size("mp"))]


def plane_ring(size):
    return [0, 1, 3, 2, 6, 7, 5, 4] if size == 8 else list(range(size))


def reduce_weight_grads(parts):
    groups = [plane_ring(lax.axis_size("dp"))]
    mine = lax.psum_scatter(parts, "dp", scatter_dimension=0, axis_index_groups=groups, tiled=False)
    return lax.optimization_barrier(mine)


def message_kernel(taps_ref, weights_ref, own_ref, *message_refs):
    taps = jnp.sum(as_float(taps_ref[...]), axis=0)
    own_ref[...] = jnp.concatenate([taps, as_float(weights_ref[0])], axis=0)
    for s, ref in enumerate(message_refs):
        ref[...] = jnp.concatenate([taps, as_float(weights_ref[s + 1])], axis=0).astype(jnp.bfloat16)


def total_kernel(own_ref, *refs):
    got, total_ref = refs[:-1], refs[-1]
    size = (total_ref.shape[0] - own_ref.shape[0]) // len(got)
    rows = [own_ref[...]] + [as_float(ref[...]) for ref in got]
    weights = tree_sum([x[size:] for x in rows])
    total_ref[...] = jnp.concatenate([x[:size] for x in rows] + [weights], axis=0).astype(jnp.bfloat16)


def reduce_rest(taps, weights):
    places, size, count = lax.axis_size("mp"), taps.shape[1], weights.shape[1]
    vmem = pl.BlockSpec(memory_space=pltpu.VMEM)
    rows = lambda n, kind: jax.ShapeDtypeStruct((n, D), kind)
    own, *messages = pl.pallas_call(
        message_kernel,
        in_specs=[vmem] * 2,
        out_specs=[vmem] * places,
        out_shape=[rows(size + count, jnp.float32)] + [rows(size + count, jnp.bfloat16)] * (places - 1),
        compiler_params=pltpu.CompilerParams(vmem_limit_bytes=SMALL_VMEM),
        name="messages",
    )(taps, weights)
    got = swap_places(messages)
    mine = pl.pallas_call(
        total_kernel,
        in_specs=[vmem] * places,
        out_specs=vmem,
        out_shape=rows(places * size + count, jnp.bfloat16),
        compiler_params=pltpu.CompilerParams(vmem_limit_bytes=SMALL_VMEM),
        name="totals",
    )(own, *got)
    mine = [mine] + [swap(mine, "dp", s) for s in plane_steps()]
    return mine, [swap(x, "dp", 1) for x in mine]


def on_device(
    image_rows, tall_weight, wide_weight, small_weight, tall_mask, wide_mask, small_mask,
    bn_gain, bn_bias, ln_gain, ln_bias, fc1_weight, fc1_bias, fc2_weight, fc2_bias, layer_scale, out_grad,
):
    rows = image_rows.shape[0]
    total = rows * lax.axis_size("dp") * lax.axis_size("mp")
    tables = tuple(jnp.asarray(t) for t in transform_tables())
    turn = lambda x: jnp.swapaxes(x, 0, 1)
    masks = (turn(tall_mask), wide_mask, small_mask)
    first = first_weights(fc1_weight, fc2_weight)

    conv, khat, moments = conv_forward(
        image_rows, (turn(tall_weight), wide_weight, small_weight), masks, tables
    )
    khat, first = lax.optimization_barrier((khat, first))
    early = {s: swap(x, "dp", 1) for s, x in first.items()}
    moments, direct, early = lax.optimization_barrier((exchange(moments), other_weights(first), early))
    other = [early[s + 1] if s + 1 in early else swap(x, "dp", 1) for s, x in enumerate(direct)]
    block_out, dbn, gw, bn_sums, vec = mlp(
        total, conv, image_rows, out_grad, moments,
        (bn_gain, bn_bias, ln_gain, ln_bias, fc2_bias, layer_scale, fc1_bias),
        (fc1_weight, fc2_weight), direct, other,
    )
    bn_sums = exchange(bn_sums)
    weights = reduce_weight_grads(gw)
    product, taps = gradient_spectra(total, dbn, conv, image_rows, khat, moments, bn_sums, vec, bn_gain, tables)
    in_grad = image_gradient(product, out_grad, tables)
    taps, in_grad = lax.optimization_barrier((exchange(taps), in_grad))
    mine, other = reduce_rest(taps, weights)
    tall_grad, wide_grad, small_grad, fc1_grad, fc2_grad, *vec = finish(mine, other, masks, bn_sums)
    tall_grad = turn(tall_grad)
    return (
        block_out, in_grad, tall_grad, wide_grad, small_grad, vec[0], vec[1], vec[2], vec[3],
        fc1_grad, vec[6], fc2_grad, vec[5], vec[4],
    )


def solution(mesh):
    rows, none = P(("dp", "mp"), None), P()
    return jax.shard_map(
        on_device,
        mesh=mesh,
        in_specs=(rows,) + (none,) * 10 + (P(None, "mp"), none, P("mp", None), none, none, rows),
        out_specs=(rows, rows) + (none,) * 7 + (P(None, "mp"), P("mp"), P("mp", None), none, none),
        check_vma=False,
    )
```

```python
import jax
import jax.numpy as jnp
import numpy as np
from jax import lax
from jax.experimental import pallas as pl
from jax.experimental.pallas import tpu as pltpu
from jax.sharding import PartitionSpec as P

MAP = 14
PIX = MAP * MAP
D = 384
LONG_LO = 25 - (MAP - 1)
SPAN = 2 * MAP - 1
BN_EPS = 1e-05
LN_EPS = 1e-06

NFREQ = 368
FROWS = 2 * NFREQ
GROUP = 4 * PIX
STEP = 2 * GROUP
WIN = 208
WIN_AT = tuple(16 * (PIX * m // 16) for m in range(4))
NTAPS = 256
REST = 245
SIDE = MAP - 3

TILE = 448
CHUNK = 256
GELU_ROWS = 64
NORM_ROWS = 112
LAST_ROWS = 112
SET = 13
FREQ_ROWS = 16
VMEM_LIMIT = 60 * 1024 * 1024
SMALL_VMEM = 4 * 1024 * 1024
FINISH_VMEM = 12 * 1024 * 1024


def tap_offsets():
    taps = [(a, b) for b in range(-2, 3) for a in range(1 - MAP, MAP)]
    for a in range(-2, 3):
        taps += [(a, b) for b in range(1 - MAP, MAP) if abs(b) > 2]
    return np.array(taps)


def bf16_pair(x):
    high = np.asarray(x, np.float32).astype(jnp.bfloat16)
    low = (np.asarray(x, np.float64) - high.astype(np.float64)).astype(np.float32).astype(jnp.bfloat16)
    return np.stack([high, low])


def transform_tables():
    freq = [
        (u, v)
        for u in range(SPAN)
        for v in range(SPAN)
        if (u, v) <= ((-u) % SPAN, (-v) % SPAN)
    ]
    freq = np.array(freq)
    count = len(freq)
    twice = np.where((freq == 0).all(axis=1), 1.0, 2.0)

    def angles(points):
        return 2 * np.pi * ((freq @ points.T) % SPAN) / SPAN

    pixels = np.stack([np.repeat(np.arange(MAP), MAP), np.tile(np.arange(MAP), MAP)], axis=1)
    theta = angles(pixels)
    forward = np.zeros((4, FROWS, WIN))
    for m in range(4):
        at = PIX * m - WIN_AT[m]
        forward[m, :count, at : at + PIX] = np.cos(theta)
        forward[m, NFREQ : NFREQ + count, at : at + PIX] = -np.sin(theta)
    inverse = np.zeros((PIX, FROWS))
    inverse[:, :count] = twice * np.cos(theta).T
    inverse[:, NFREQ : NFREQ + count] = -twice * np.sin(theta).T
    taps = tap_offsets()
    phi = angles(taps)
    from_taps = np.zeros((FROWS, NTAPS))
    from_taps[:count, : len(taps)] = np.cos(phi)
    from_taps[NFREQ : NFREQ + count, : len(taps)] = np.sin(phi)
    to_taps = np.zeros((NTAPS, FROWS))
    to_taps[: len(taps), :count] = twice * np.cos(phi).T
    to_taps[: len(taps), NFREQ : NFREQ + count] = twice * np.sin(phi).T
    as_bf16 = lambda x: x.astype(np.float32).astype(jnp.bfloat16)
    return as_bf16(forward), as_bf16(inverse), bf16_pair(from_taps), bf16_pair(to_taps)


def dot(a, b):
    return jnp.dot(a, b, preferred_element_type=jnp.float32)


def dot_t(a, b):
    return lax.dot_general(a, b, (((1,), (1,)), ((), ())), preferred_element_type=jnp.float32)


def as_float(x):
    return x.astype(jnp.float32)


def as_row(ref):
    return ref[...].reshape(1, -1)


def fold8(x):
    return jnp.sum(x.reshape(-1, 8, x.shape[-1]), axis=0)


def pair_window(ref, m):
    return jnp.concatenate(
        [ref[g * GROUP + WIN_AT[m] : g * GROUP + WIN_AT[m] + WIN, :] for g in range(2)],
        axis=1,
    )


def put_pair(ref, m, pair):
    for g in range(2):
        at = g * GROUP + PIX * m
        ref[at : at + PIX, :] = pair[:, g * D : (g + 1) * D]


def whole(a):
    return pl.BlockSpec(a.shape, lambda i, n=len(a.shape): (0,) * n)


def start_all(copies):
    for copy in copies:
        copy.start()


def wait_all(copies):
    for copy in copies:
        copy.wait()


def conv_kernel(
    image_ref, tall_ref, wide_ref, small_ref, tall_mask_ref, wide_mask_ref, small_mask_ref,
    forward_ref, inverse_ref, from_taps_ref,
    conv_ref, khat_ref, moments_ref,
    product_ref, taps_ref, sums_ref,
):
    step = pl.program_id(0)

    @pl.when(step == 0)
    def _():
        sums_ref[...] = jnp.zeros_like(sums_ref)
        taps_ref[...] = jnp.zeros_like(taps_ref)
        for b in range(5):
            column = tall_ref[b, LONG_LO : LONG_LO + SPAN] * as_float(tall_mask_ref[b, LONG_LO : LONG_LO + SPAN])
            middle = column[MAP - 3 : MAP + 2] + wide_ref[:, 23 + b, :] * as_float(wide_mask_ref[:, 23 + b, :])
            middle = middle + small_ref[:, b, :] * as_float(small_mask_ref[:, b, :])
            taps_ref[SPAN * b : SPAN * b + SPAN, :] = column
            taps_ref[SPAN * b + MAP - 3 : SPAN * b + MAP + 2, :] = middle
        for r in range(5):
            at = 5 * SPAN + 2 * SIDE * r
            for lo in (LONG_LO, 28):
                row = wide_ref[r, lo : lo + SIDE] * as_float(wide_mask_ref[r, lo : lo + SIDE])
                taps_ref[at : at + SIDE, :] = row
                at += SIDE
        taps = taps_ref[...].astype(jnp.bfloat16)
        khat = dot(from_taps_ref[0], taps) + dot(from_taps_ref[1], taps)
        khat_ref[...] = khat * np.float32(1.0 / (SPAN * SPAN))

    for k in range(2):
        images = (2 * k, 2 * k + 1)
        spectra = [dot(forward_ref[m], pair_window(image_ref, m)) for m in images]
        for r in range(0, NFREQ, FREQ_ROWS):
            re, im = slice(r, r + FREQ_ROWS), slice(NFREQ + r, NFREQ + r + FREQ_ROWS)
            real, imag = khat_ref[re, :], khat_ref[im, :]
            for m, xhat in zip(images, spectra):
                for g in range(2):
                    cols = slice(g * D, (g + 1) * D)
                    xr, xi = xhat[re, cols], xhat[im, cols]
                    product_ref[m, re, cols] = (real * xr - imag * xi).astype(jnp.bfloat16)
                    product_ref[m, im, cols] = (real * xi + imag * xr).astype(jnp.bfloat16)
        for m in images:
            put_pair(conv_ref, m, dot(inverse_ref[...], product_ref[m]))
    conv = conv_ref[...]
    sums_ref[:8, :] += fold8(conv)
    sums_ref[8:, :] += fold8(conv * conv)

    @pl.when(step == pl.num_programs(0) - 1)
    def _():
        sums = [jnp.sum(sums_ref[8 * i : 8 * i + 8, :], axis=0, keepdims=True) for i in range(2)]
        put_everywhere(moments_ref, jnp.concatenate(sums, axis=0))


def conv_forward(image_rows, weights, masks, tables):
    rows = image_rows.shape[0]
    steps = rows // STEP
    forward, inverse, from_taps, _ = tables
    khat = jax.ShapeDtypeStruct((FROWS, D), jnp.float32)
    devices = lax.axis_size("dp") * lax.axis_size("mp")
    moments = jax.ShapeDtypeStruct((devices, 2, D), jnp.float32)
    return pl.pallas_call(
        conv_kernel,
        grid=(steps,),
        in_specs=[pl.BlockSpec((STEP, D), lambda i: (i, 0))]
        + [whole(a) for a in (*weights, *masks, forward, inverse, from_taps)],
        out_specs=[
            pl.BlockSpec((STEP, D), lambda i: (i, 0)),
            whole(khat),
            whole(moments),
        ],
        out_shape=[
            jax.ShapeDtypeStruct((rows, D), jnp.float32),
            khat,
            moments,
        ],
        scratch_shapes=[
            pltpu.VMEM((4, FROWS, 2 * D), jnp.bfloat16),
            pltpu.VMEM((NTAPS, D), jnp.float32),
            pltpu.VMEM((16, D), jnp.float32),
        ],
        compiler_params=pltpu.CompilerParams(vmem_limit_bytes=VMEM_LIMIT),
        cost_estimate=pl.CostEstimate(
            flops=4 * rows * D * FROWS, bytes_accessed=rows * D * 10, transcendentals=0
        ),
        name="conv_forward",
    )(image_rows, *weights, *masks, forward, inverse, from_taps)


def put_everywhere(ref, rows):
    ref[...] = jnp.broadcast_to(rows[None], ref.shape)


def arrived(ref):
    return jnp.sum(ref[...], axis=0)


def exchange(x):
    return lax.all_to_all(x, ("dp", "mp"), split_axis=0, concat_axis=0)


def batch_norm_terms(moments_ref, total):
    moments = arrived(moments_ref)
    mean = moments[0:1, :] * np.float32(1.0 / total)
    variance = moments[1:2, :] * np.float32(1.0 / total) - mean * mean
    return mean, lax.rsqrt(variance + BN_EPS)


def split_refs(refs):
    return (*refs[:3], refs[3 : 3 + SET], refs[3 + SET : 3 + 2 * SET], *refs[3 + 2 * SET :])


def mlp_kernel(total, *refs):
    blocks = lax.axis_size("mp")
    conv_hbm, image_hbm, grad_hbm, moments_ref = refs[:4]
    vectors, refs = [as_row(ref) for ref in refs[4:11]], refs[11:]
    own, direct, other = refs[:2], refs[2 : 1 + blocks], refs[1 + blocks : 2 * blocks]
    out_hbm, dbn_hbm, gw_hbm, bn_sums_ref, vec_ref = refs[2 * blocks : 5 + 2 * blocks]
    (
        conv_all, image_all, grad_all, set_a, set_b, w1_ref, w2_ref, mixed_ref, dnormed_ref, g1_ref, g2_ref,
        gw_ref, sum_ref, tile_sems, weight_sems, gw_sems,
    ) = split_refs(refs[5 + 2 * blocks :])
    rows = conv_all.shape[0]
    tiles = rows // TILE
    hidden = blocks * D
    core, place = lax.axis_index("dp") % 2, lax.axis_index("mp")

    def rows_of_tile(t):
        return pl.ds(pl.multiple_of(t * TILE, TILE), TILE)

    def reads(t):
        at = rows_of_tile(t)
        pairs = [(conv_hbm, conv_all), (grad_hbm, grad_all), (image_hbm, image_all)]
        return [
            pltpu.make_async_copy(a.at[at], b.at[at], tile_sems.at[i, t]) for i, (a, b) in enumerate(pairs)
        ]

    def writes(t, buffers):
        at = rows_of_tile(t)
        pairs = [(buffers[3], out_hbm), (buffers[4], dbn_hbm)]
        return [
            pltpu.make_async_copy(a, b.at[at], tile_sems.at[3 + i, t]) for i, (a, b) in enumerate(pairs)
        ]

    start_all(reads(0))

    def weight_copies(first, second):
        copies = []
        for s in range(blocks):
            at = slice(s * D, (s + 1) * D)
            source = (own[0], own[1]) if s == 0 else (first[s - 1], second[s - 1])
            copies.append(pltpu.make_async_copy(source[0], w1_ref.at[:, at], weight_sems.at[0, s]))
            copies.append(pltpu.make_async_copy(source[1], w2_ref.at[at, :], weight_sems.at[1, s]))
        return copies

    @pl.when(core == 0)
    def _():
        start_all(weight_copies(direct, other))

    @pl.when(core != 0)
    def _():
        start_all(weight_copies(other, direct))

    for t in range(1, tiles):
        start_all(reads(t))

    mean, bn_inv = batch_norm_terms(moments_ref, total)
    bn_gain, bn_bias, ln_gain, ln_bias, fc2_bias, layer_scale, fc1_bias = vectors
    scale = bn_inv * bn_gain
    bias_of = [fc1_bias[:, i * D : (i + 1) * D] for i in range(blocks)]
    bias = jnp.concatenate(
        [sum(jnp.where((place ^ s) == i, bias_of[i], 0.0) for i in range(blocks)) for s in range(blocks)], axis=1
    )
    sum_ref[...] = jnp.zeros_like(sum_ref)
    g1_ref[...] = jnp.zeros_like(g1_ref)
    g2_ref[...] = jnp.zeros_like(g2_ref)
    ones_row = jnp.where(lax.broadcasted_iota(jnp.int32, (16, TILE), 0) == 0, 1.0, 0.0).astype(jnp.bfloat16)
    set_a[7][D:, :] = ones_row
    set_b[7][D:, :] = ones_row

    def wide(x):
        return jnp.broadcast_to(x, (x.shape[0], 128))

    def across(x):
        return jnp.concatenate([x] * (D // 128), axis=1)

    def fetch(t, buffers):
        wait_all(reads(t))
        at = rows_of_tile(t)
        for whole, buffer in zip((conv_all, grad_all, image_all), buffers):
            buffer[...] = whole[at, :]

    def normalize(buffers):
        conv_ref, grad_ref = buffers[:2]
        normed_ref, dproj_ref, normed_t_ref, dproj_t_ref, mu_ref, inv_ref = buffers[5:11]
        for r in range(0, TILE, NORM_ROWS):
            at = slice(r, r + NORM_ROWS)
            out = (conv_ref[at, :] - mean) * scale + bn_bias
            mu = jnp.mean(out, axis=1, keepdims=True)
            center = out - mu
            inv = lax.rsqrt(jnp.mean(center * center, axis=1, keepdims=True) + LN_EPS)
            mu_ref[at, :] = wide(mu)
            inv_ref[at, :] = wide(inv)
            normed_ref[at, :] = (center * inv * ln_gain + ln_bias).astype(jnp.bfloat16)
            grad = as_float(grad_ref[at, :])
            dproj_ref[at, :] = (grad * layer_scale).astype(jnp.bfloat16)
            sum_ref[40:48, :] += fold8(grad)
        normed_t_ref[:D, :] = jnp.transpose(normed_ref[...])
        dproj_t_ref[...] = jnp.transpose(dproj_ref[...])

    root = np.float32(np.sqrt(2.0 / np.pi))
    cubic = np.float32(0.044715 * np.sqrt(2.0 / np.pi))

    def gelu_chunk(c, buffers):
        normed_ref, dproj_ref, act_ref, dhid_ref = buffers[5], buffers[6], buffers[11], buffers[12]
        cols = slice(c * CHUNK, (c + 1) * CHUNK)
        hid_all = dot(normed_ref[...], w1_ref[:, cols])
        dact_all = dot_t(dproj_ref[...], w2_ref[cols, :])
        for r in range(0, TILE, GELU_ROWS):
            hid = hid_all[r : r + GELU_ROWS] + bias[:, cols]
            square = hid * hid
            th = jnp.tanh(hid * (root + cubic * square))
            half = 0.5 + 0.5 * th
            act = hid * half
            slope = half + act * (1.0 - th) * (root + 3 * cubic * square)
            act_ref[r : r + GELU_ROWS, cols] = act.astype(jnp.bfloat16)
            dhid_ref[r : r + GELU_ROWS, cols] = (dact_all[r : r + GELU_ROWS] * slope).astype(jnp.bfloat16)

    def finish_rows(r, buffers):
        conv_ref, grad_ref, image_ref, out_ref, dbn_ref = buffers[:5]
        mu_ref, inv_ref = buffers[9:11]
        at = slice(r, r + LAST_ROWS)
        mixed = mixed_ref[at, :] + fc2_bias
        dnormed = dnormed_ref[at, :]
        out_ref[at, :] = (as_float(image_ref[at, :]) + layer_scale * mixed).astype(jnp.bfloat16)
        conv = conv_ref[at, :] - mean
        bn_hat = conv * bn_inv
        inv = across(inv_ref[at, :])
        ln_hat = (conv * scale + bn_bias - across(mu_ref[at, :])) * inv
        d_hat = dnormed * ln_gain
        first = jnp.mean(d_hat, axis=1, keepdims=True)
        second = jnp.mean(d_hat * ln_hat, axis=1, keepdims=True)
        dbn = inv * (d_hat - first - ln_hat * second)
        dbn_ref[at, :] = dbn.astype(jnp.bfloat16)
        sum_ref[0:8, :] += fold8(dbn * bn_hat)
        sum_ref[8:16, :] += fold8(dbn)
        sum_ref[16:24, :] += fold8(dnormed * ln_hat)
        sum_ref[24:32, :] += fold8(dnormed)
        sum_ref[32:40, :] += fold8(as_float(grad_ref[at, :]) * mixed)

    chunks = hidden // CHUNK
    parts = TILE // LAST_ROWS

    def step(ahead, now):
        if now is not None:
            act_ref, dhid_ref = now[11:13]
            mixed_ref[...] = dot(act_ref[...], w2_ref[...])
            dnormed_ref[...] = dot_t(dhid_ref[...], w1_ref[...])
        if ahead is not None:
            normalize(ahead)
        for c in range(chunks):
            if ahead is not None:
                gelu_chunk(c, ahead)
            if now is not None:
                cols = slice(c * CHUNK, (c + 1) * CHUNK)
                g1_ref[:, cols] += dot(now[7][...], dhid_ref[:, cols])
                g2_ref[:, cols] += dot(now[8][...], act_ref[:, cols])
                for i in range(c * parts // chunks, (c + 1) * parts // chunks):
                    finish_rows(i * LAST_ROWS, now)

    def two_steps(i, _):
        fetch(2 * i + 1, set_b)

        @pl.when(i > 0)
        def _():
            wait_all(writes(2 * i - 2, set_a))

        step(set_b, set_a)
        start_all(writes(2 * i, set_a))
        fetch(2 * i + 2, set_a)

        @pl.when(i > 0)
        def _():
            wait_all(writes(2 * i - 1, set_b))

        step(set_a, set_b)
        start_all(writes(2 * i + 1, set_b))
        return 0

    fetch(0, set_a)
    wait_all(weight_copies(direct, other))
    step(set_a, None)
    lax.fori_loop(0, (tiles - 1) // 2, two_steps, 0)
    last = tiles - 1
    if tiles % 2 == 0:
        fetch(last, set_b)
        if tiles > 2:
            wait_all(writes(last - 3, set_a))
        step(set_b, set_a)
        start_all(writes(last - 1, set_a))
        if tiles > 2:
            wait_all(writes(last - 2, set_b))
        step(None, set_b)
        start_all(writes(last, set_b))
    else:
        if tiles > 1:
            wait_all(writes(last - 2, set_a))
        step(None, set_a)
        start_all(writes(last, set_a))

    chips, size = gw_ref.shape[1] // 2, gw_ref.shape[2]
    ring = plane_ring(2 * chips)
    gw_copy = lambda s: pltpu.make_async_copy(gw_ref.at[s], gw_hbm.at[:, s], gw_sems.at[s])
    for s in range(blocks):
        cols = slice(s * D, (s + 1) * D)
        vec_ref[pl.ds(4 + (place ^ s), 1), :] = g1_ref[D : D + 1, cols]
        for i in range(chips):
            rows_of = slice(i * size, (i + 1) * size)
            gw_ref[s, ring.index(2 * i)] = g1_ref[rows_of, cols].astype(jnp.bfloat16)
            gw_ref[s, ring.index(2 * i + 1)] = g2_ref[rows_of, cols].astype(jnp.bfloat16)
        gw_copy(s).start()

    sums = [jnp.sum(sum_ref[8 * i : 8 * i + 8, :], axis=0, keepdims=True) for i in range(6)]
    put_everywhere(bn_sums_ref, jnp.concatenate(sums[:2], axis=0))
    vec_ref[0:4, :] = jnp.concatenate(sums[2:5] + [sums[5] * layer_scale], axis=0)
    for s in range(blocks):
        gw_copy(s).wait()
    first_set, second_set = (set_a, set_b) if tiles % 2 == 1 else (set_b, set_a)
    if tiles > 1:
        wait_all(writes(last - 1, second_set))
    wait_all(writes(last, first_set))


def mlp(total, conv, image_rows, out_grad, moments, vectors, own, direct, other):
    rows = conv.shape[0]
    tiles = rows // TILE
    blocks, chips = lax.axis_size("mp"), lax.axis_size("dp") // 2
    hidden = blocks * D
    vmem, hbm = pl.BlockSpec(memory_space=pltpu.VMEM), pl.BlockSpec(memory_space=pl.ANY)
    f32, bf16 = jnp.float32, jnp.bfloat16
    return pl.pallas_call(
        lambda *refs: mlp_kernel(total, *refs),
        in_specs=[hbm] * 3 + [vmem] * 8 + [hbm] * (2 * blocks),
        out_specs=[hbm] * 3 + [vmem] * 2,
        out_shape=[
            jax.ShapeDtypeStruct((rows, D), bf16),
            jax.ShapeDtypeStruct((rows, D), bf16),
            jax.ShapeDtypeStruct((2 * chips, blocks, D // chips, D), bf16),
            jax.ShapeDtypeStruct((2 * chips * blocks, 2, D), f32),
            jax.ShapeDtypeStruct((4 + blocks, D), f32),
        ],
        scratch_shapes=[
            pltpu.VMEM((rows, D), f32),
            pltpu.VMEM((rows, D), bf16),
            pltpu.VMEM((rows, D), bf16),
        ]
        + [
            pltpu.VMEM((TILE, D), f32),
            pltpu.VMEM((TILE, D), bf16),
            pltpu.VMEM((TILE, D), bf16),
            pltpu.VMEM((TILE, D), bf16),
            pltpu.VMEM((TILE, D), bf16),
            pltpu.VMEM((TILE, D), bf16),
            pltpu.VMEM((TILE, D), bf16),
            pltpu.VMEM((D + 16, TILE), bf16),
            pltpu.VMEM((D, TILE), bf16),
            pltpu.VMEM((TILE, 128), f32),
            pltpu.VMEM((TILE, 128), f32),
            pltpu.VMEM((TILE, hidden), bf16),
            pltpu.VMEM((TILE, hidden), bf16),
        ]
        * 2
        + [pltpu.VMEM((D, hidden), bf16), pltpu.VMEM((hidden, D), bf16)]
        + [pltpu.VMEM((TILE, D), f32)] * 2
        + [
            pltpu.VMEM((D + 16, hidden), f32),
            pltpu.VMEM((D, hidden), f32),
            pltpu.VMEM((blocks, 2 * chips, D // chips, D), bf16),
            pltpu.VMEM((48, D), f32),
            pltpu.SemaphoreType.DMA((5, tiles)),
            pltpu.SemaphoreType.DMA((2, blocks)),
            pltpu.SemaphoreType.DMA((blocks,)),
        ],
        compiler_params=pltpu.CompilerParams(vmem_limit_bytes=VMEM_LIMIT),
        cost_estimate=pl.CostEstimate(
            flops=12 * rows * D * hidden, bytes_accessed=rows * D * 20, transcendentals=rows * hidden
        ),
        name="mlp",
    )(conv, image_rows, out_grad, moments, *vectors, *own, *direct, *other)


def spectra_kernel(
    total, dbn_ref, conv_ref, image_ref, khat_ref, moments_ref, bn_sums_ref, vec_ref, bn_gain_ref,
    forward_ref, to_taps_ref,
    product_ref, taps_ref,
    dconv_ref, dhat_ref, all_taps_ref,
):
    step = pl.program_id(0)
    mean, bn_inv = batch_norm_terms(moments_ref, total)
    bn_sums = arrived(bn_sums_ref) * np.float32(1.0 / total)
    gain = as_row(bn_gain_ref) * bn_inv
    slope, shift = bn_sums[0:1, :], bn_sums[1:2, :]

    @pl.when(step == 0)
    def _():
        dhat_ref[...] = jnp.zeros_like(dhat_ref)

    for r in range(0, STEP, LAST_ROWS):
        at = slice(r, r + LAST_ROWS)
        bn_hat = (conv_ref[at, :] - mean) * bn_inv
        dconv = gain * (as_float(dbn_ref[at, :]) - shift - bn_hat * slope)
        dconv_ref[at, :] = dconv.astype(jnp.bfloat16)
    for k in range(2):
        images = (2 * k, 2 * k + 1)
        spectra = [dot(forward_ref[m], pair_window(dconv_ref, m)) for m in images]
        image_spectra = [dot(forward_ref[m], pair_window(image_ref, m)) for m in images]
        for r in range(0, NFREQ, FREQ_ROWS):
            re, im = slice(r, r + FREQ_ROWS), slice(NFREQ + r, NFREQ + r + FREQ_ROWS)
            real, imag = khat_ref[re, :], khat_ref[im, :]
            tap_re, tap_im = [], []
            for m, ghat, xhat in zip(images, spectra, image_spectra):
                for g in range(2):
                    cols = slice(g * D, (g + 1) * D)
                    gr, gi = ghat[re, cols], ghat[im, cols]
                    product_ref[m, re, cols] = (real * gr + imag * gi).astype(jnp.bfloat16)
                    product_ref[m, im, cols] = (real * gi - imag * gr).astype(jnp.bfloat16)
                    xr, xi = xhat[re, cols], xhat[im, cols]
                    tap_re.append(xr * gr + xi * gi)
                    tap_im.append(xr * gi - xi * gr)
            dhat_ref[re, :] += tree_sum(tap_re)
            dhat_ref[im, :] += tree_sum(tap_im)

    @pl.when(step == pl.num_programs(0) - 1)
    def _():
        dhat = dhat_ref[...]
        high = dhat.astype(jnp.bfloat16)
        low = (dhat - as_float(high)).astype(jnp.bfloat16)
        taps = dot(to_taps_ref[0], high) + dot(to_taps_ref[0], low) + dot(to_taps_ref[1], high)
        all_taps_ref[...] = taps * np.float32(1.0 / (SPAN * SPAN))
        all_taps_ref[REST : REST + vec_ref.shape[0], :] = vec_ref[...]
        devices, size, _ = taps_ref.shape
        for i in range(devices):
            if i * size < NTAPS:
                taps_ref[i] = all_taps_ref[i * size : (i + 1) * size, :].astype(jnp.bfloat16)
            else:
                taps_ref[i] = jnp.zeros((size, D), jnp.bfloat16)


def gradient_spectra(total, dbn, conv, image_rows, khat, moments, bn_sums, vec, bn_gain, tables):
    rows = conv.shape[0]
    steps = rows // STEP
    forward, _, _, to_taps = tables
    devices = lax.axis_size("dp") * lax.axis_size("mp")
    f32, bf16 = jnp.float32, jnp.bfloat16
    block = pl.BlockSpec((STEP, D), lambda i: (i, 0))
    spectra = pl.BlockSpec((4, FROWS, 2 * D), lambda i: (i, 0, 0))
    taps = jax.ShapeDtypeStruct((devices, max(8, NTAPS // devices), D), bf16)
    return pl.pallas_call(
        lambda *refs: spectra_kernel(total, *refs),
        grid=(steps,),
        in_specs=[block] * 3
        + [whole(a) for a in (khat, moments, bn_sums, vec, bn_gain, forward, to_taps)],
        out_specs=[spectra, whole(taps)],
        out_shape=[jax.ShapeDtypeStruct((4 * steps, FROWS, 2 * D), bf16), taps],
        scratch_shapes=[
            pltpu.VMEM((STEP, D), bf16),
            pltpu.VMEM((FROWS, D), f32),
            pltpu.VMEM((NTAPS, D), f32),
        ],
        compiler_params=pltpu.CompilerParams(vmem_limit_bytes=VMEM_LIMIT),
        cost_estimate=pl.CostEstimate(
            flops=2 * rows * D * FROWS, bytes_accessed=rows * D * 26, transcendentals=0
        ),
        name="gradient_spectra",
    )(dbn, conv, image_rows, khat, moments, bn_sums, vec, bn_gain, forward, to_taps)


def inverse_kernel(product_ref, grad_ref, inverse_ref, in_grad_ref, image_grad_ref):
    for m in range(4):
        put_pair(image_grad_ref, m, dot(inverse_ref[...], product_ref[m]))
    in_grad_ref[...] = (image_grad_ref[...] + as_float(grad_ref[...])).astype(jnp.bfloat16)


def image_gradient(product, out_grad, tables):
    rows = out_grad.shape[0]
    inverse = tables[1]
    block = pl.BlockSpec((STEP, D), lambda i: (i, 0))
    return pl.pallas_call(
        inverse_kernel,
        grid=(rows // STEP,),
        in_specs=[pl.BlockSpec((4, FROWS, 2 * D), lambda i: (i, 0, 0)), block, whole(inverse)],
        out_specs=block,
        out_shape=jax.ShapeDtypeStruct((rows, D), jnp.bfloat16),
        scratch_shapes=[pltpu.VMEM((STEP, D), jnp.float32)],
        compiler_params=pltpu.CompilerParams(vmem_limit_bytes=VMEM_LIMIT),
        cost_estimate=pl.CostEstimate(
            flops=2 * rows * D * FROWS, bytes_accessed=rows * D * 10, transcendentals=0
        ),
        name="image_gradient",
    )(product, out_grad, inverse)


def finish_kernel(chips, *refs):
    mine, other = refs[:chips], refs[chips : 2 * chips]
    tall_mask_ref, wide_mask_ref, small_mask_ref, bn_sums_ref = refs[2 * chips : 2 * chips + 4]
    tall_ref, wide_ref, small_ref, fc1_ref, fc2_ref = refs[2 * chips + 4 : 2 * chips + 9]
    vector_refs, taps_ref, fc2_t_ref = refs[2 * chips + 9 : -2], refs[-2], refs[-1]
    core, chip = lax.axis_index("dp") % 2, lax.axis_index("dp") // 2
    places, place = lax.axis_size("mp"), lax.axis_index("mp")
    size, count = taps_ref.shape[0] // (2 * chips * places), D // chips
    for k in range(chips):
        at = pl.ds(pl.multiple_of((chip ^ k) * count, 8), count)
        mine_rows, other_rows = as_float(mine[k][...]), as_float(other[k][...])
        for s in range(places):
            for owner, rows in ((core, mine_rows), (1 - core, other_rows)):
                device = (2 * (chip ^ k) + owner) * places + (place ^ s)
                taps_ref[pl.ds(pl.multiple_of(device * size, 8), size), :] = rows[s * size : (s + 1) * size]

        @pl.when(core == 0)
        def _():
            fc1_ref[at, :] = mine_rows[places * size :]
            fc2_t_ref[at, :] = other_rows[places * size :]

        @pl.when(core != 0)
        def _():
            fc1_ref[at, :] = other_rows[places * size :]
            fc2_t_ref[at, :] = mine_rows[places * size :]

    fc2_ref[...] = jnp.transpose(fc2_t_ref[...])
    bn_sums = arrived(bn_sums_ref)
    rows = [bn_sums[0:1], bn_sums[1:2]] + [taps_ref[REST + i : REST + i + 1, :] for i in range(4)]
    rows.append(taps_ref[pl.ds(REST + 4 + place, 1), :])
    for ref, row in zip(vector_refs, rows):
        ref[...] = row.reshape(ref.shape)
    tall_ref[...] = jnp.zeros_like(tall_ref)
    wide_ref[...] = jnp.zeros_like(wide_ref)
    for b in range(5):
        column = taps_ref[SPAN * b : SPAN * b + SPAN, :]
        middle = column[MAP - 3 : MAP + 2, :]
        tall_ref[b, LONG_LO : LONG_LO + SPAN] = column * as_float(tall_mask_ref[b, LONG_LO : LONG_LO + SPAN])
        small_ref[:, b, :] = middle * as_float(small_mask_ref[:, b, :])
        wide_ref[:, 23 + b, :] = middle * as_float(wide_mask_ref[:, 23 + b, :])
    for r in range(5):
        at = 5 * SPAN + 2 * SIDE * r
        for lo in (LONG_LO, 28):
            wide_ref[r, lo : lo + SIDE] = taps_ref[at : at + SIDE, :] * as_float(wide_mask_ref[r, lo : lo + SIDE])
            at += SIDE


def finish(mine, other, masks, bn_sums):
    chips, places = len(mine), lax.axis_size("mp")
    size = (mine[0].shape[0] - D // chips) // places
    vmem = pl.BlockSpec(memory_space=pltpu.VMEM)
    square = jax.ShapeDtypeStruct((D, D), jnp.float32)
    return pl.pallas_call(
        lambda *refs: finish_kernel(chips, *refs),
        in_specs=[vmem] * (2 * chips + 4),
        out_specs=[vmem] * 12,
        out_shape=[jax.ShapeDtypeStruct(m.shape, jnp.float32) for m in masks] + [square, square]
        + [jax.ShapeDtypeStruct((D,), jnp.float32)] * 7,
        scratch_shapes=[pltpu.VMEM((2 * chips * places * size, D), jnp.float32), pltpu.VMEM((D, D), jnp.float32)],
        compiler_params=pltpu.CompilerParams(vmem_limit_bytes=FINISH_VMEM),
        name="finish",
    )(*mine, *other, *masks, bn_sums)


def swap(x, axis, bit):
    size = lax.axis_size(axis)
    return lax.ppermute(x, axis, [(i, i ^ bit) for i in range(size)])


def swap_places(parts):
    got = [swap(x, "mp", s + 1) for s, x in reversed(list(enumerate(parts)))]
    return got[::-1]


def tree_sum(terms):
    while len(terms) > 1:
        terms = [a + b for a, b in zip(terms[::2], terms[1::2])]
    return terms[0]


def plane_steps():
    return range(2, lax.axis_size("dp"), 2)


def first_weights(fc1_weight, fc2_weight):
    mine = jnp.where(lax.axis_index("dp") % 2 == 0, fc1_weight, fc2_weight)
    powers = [1 << i for i in range(lax.axis_size("mp").bit_length() - 1)]
    return {s: swap(mine, "mp", s) for s in reversed(powers)}


def other_weights(got):
    for s in range(1, lax.axis_size("mp")):
        if s not in got:
            high = 1 << (s.bit_length() - 1)
            got[s] = swap(got[high], "mp", s ^ high)
    return [got[s] for s in range(1, lax.axis_size("mp"))]


def plane_ring(size):
    return [0, 1, 3, 2, 6, 7, 5, 4] if size == 8 else list(range(size))


def reduce_weight_grads(parts):
    groups = [plane_ring(lax.axis_size("dp"))]
    mine = lax.psum_scatter(parts, "dp", scatter_dimension=0, axis_index_groups=groups, tiled=False)
    return lax.optimization_barrier(mine)


def message_kernel(taps_ref, weights_ref, own_ref, *message_refs):
    taps = jnp.sum(as_float(taps_ref[...]), axis=0)
    own_ref[...] = jnp.concatenate([taps, as_float(weights_ref[0])], axis=0)
    for s, ref in enumerate(message_refs):
        ref[...] = jnp.concatenate([taps, as_float(weights_ref[s + 1])], axis=0).astype(jnp.bfloat16)


def total_kernel(own_ref, *refs):
    got, total_ref = refs[:-1], refs[-1]
    size = (total_ref.shape[0] - own_ref.shape[0]) // len(got)
    rows = [own_ref[...]] + [as_float(ref[...]) for ref in got]
    weights = tree_sum([x[size:] for x in rows])
    total_ref[...] = jnp.concatenate([x[:size] for x in rows] + [weights], axis=0).astype(jnp.bfloat16)


def reduce_rest(taps, weights):
    places, size, count = lax.axis_size("mp"), taps.shape[1], weights.shape[1]
    vmem = pl.BlockSpec(memory_space=pltpu.VMEM)
    rows = lambda n, kind: jax.ShapeDtypeStruct((n, D), kind)
    own, *messages = pl.pallas_call(
        message_kernel,
        in_specs=[vmem] * 2,
        out_specs=[vmem] * places,
        out_shape=[rows(size + count, jnp.float32)] + [rows(size + count, jnp.bfloat16)] * (places - 1),
        compiler_params=pltpu.CompilerParams(vmem_limit_bytes=SMALL_VMEM),
        name="messages",
    )(taps, weights)
    got = swap_places(messages)
    mine = pl.pallas_call(
        total_kernel,
        in_specs=[vmem] * places,
        out_specs=vmem,
        out_shape=rows(places * size + count, jnp.bfloat16),
        compiler_params=pltpu.CompilerParams(vmem_limit_bytes=SMALL_VMEM),
        name="totals",
    )(own, *got)
    mine = [mine] + [swap(mine, "dp", s) for s in plane_steps()]
    return mine, [swap(x, "dp", 1) for x in mine]


def on_device(
    image_rows, tall_weight, wide_weight, small_weight, tall_mask, wide_mask, small_mask,
    bn_gain, bn_bias, ln_gain, ln_bias, fc1_weight, fc1_bias, fc2_weight, fc2_bias, layer_scale, out_grad,
):
    rows = image_rows.shape[0]
    total = rows * lax.axis_size("dp") * lax.axis_size("mp")
    tables = tuple(jnp.asarray(t) for t in transform_tables())
    turn = lambda x: jnp.swapaxes(x, 0, 1)
    masks = (turn(tall_mask), wide_mask, small_mask)
    first = first_weights(fc1_weight, fc2_weight)

    conv, khat, moments = conv_forward(
        image_rows, (turn(tall_weight), wide_weight, small_weight), masks, tables
    )
    khat, first = lax.optimization_barrier((khat, first))
    early = {s: swap(x, "dp", 1) for s, x in first.items()}
    moments, direct, early = lax.optimization_barrier((exchange(moments), other_weights(first), early))
    other = [early[s + 1] if s + 1 in early else swap(x, "dp", 1) for s, x in enumerate(direct)]
    block_out, dbn, gw, bn_sums, vec = mlp(
        total, conv, image_rows, out_grad, moments,
        (bn_gain, bn_bias, ln_gain, ln_bias, fc2_bias, layer_scale, fc1_bias),
        (fc1_weight, fc2_weight), direct, other,
    )
    bn_sums = exchange(bn_sums)
    weights = reduce_weight_grads(gw)
    product, taps = gradient_spectra(total, dbn, conv, image_rows, khat, moments, bn_sums, vec, bn_gain, tables)
    in_grad = image_gradient(product, out_grad, tables)
    taps, in_grad, weights = lax.optimization_barrier((exchange(taps), in_grad, weights))
    mine, other = reduce_rest(taps, weights)
    tall_grad, wide_grad, small_grad, fc1_grad, fc2_grad, *vec = finish(mine, other, masks, bn_sums)
    tall_grad = turn(tall_grad)
    return (
        block_out, in_grad, tall_grad, wide_grad, small_grad, vec[0], vec[1], vec[2], vec[3],
        fc1_grad, vec[6], fc2_grad, vec[5], vec[4],
    )


def solution(mesh):
    rows, none = P(("dp", "mp"), None), P()
    return jax.shard_map(
        on_device,
        mesh=mesh,
        in_specs=(rows,) + (none,) * 10 + (P(None, "mp"), none, P("mp", None), none, none, rows),
        out_specs=(rows, rows) + (none,) * 7 + (P(None, "mp"), P("mp"), P("mp", None), none, none),
        check_vma=False,
    )
```

```python
import jax
import jax.numpy as jnp
import numpy as np
from jax import lax
from jax.experimental import pallas as pl
from jax.experimental.pallas import tpu as pltpu
from jax.sharding import PartitionSpec as P

MAP = 14
PIX = MAP * MAP
D = 384
LONG_LO = 25 - (MAP - 1)
SPAN = 2 * MAP - 1
BN_EPS = 1e-05
LN_EPS = 1e-06

NFREQ = 368
FROWS = 2 * NFREQ
GROUP = 4 * PIX
STEP = 2 * GROUP
WIN = 208
WIN_AT = tuple(16 * (PIX * m // 16) for m in range(4))
NTAPS = 256
REST = 245
SIDE = MAP - 3

TILE = 448
CHUNK = 256
GELU_ROWS = 64
NORM_ROWS = 112
LAST_ROWS = 112
SET = 13
FREQ_ROWS = 16
VMEM_LIMIT = 60 * 1024 * 1024
SMALL_VMEM = 4 * 1024 * 1024
FINISH_VMEM = 12 * 1024 * 1024


def tap_offsets():
    taps = [(a, b) for b in range(-2, 3) for a in range(1 - MAP, MAP)]
    for a in range(-2, 3):
        taps += [(a, b) for b in range(1 - MAP, MAP) if abs(b) > 2]
    return np.array(taps)


def bf16_pair(x):
    high = np.asarray(x, np.float32).astype(jnp.bfloat16)
    low = (np.asarray(x, np.float64) - high.astype(np.float64)).astype(np.float32).astype(jnp.bfloat16)
    return np.stack([high, low])


def transform_tables():
    freq = [
        (u, v)
        for u in range(SPAN)
        for v in range(SPAN)
        if (u, v) <= ((-u) % SPAN, (-v) % SPAN)
    ]
    freq = np.array(freq)
    count = len(freq)
    twice = np.where((freq == 0).all(axis=1), 1.0, 2.0)

    def angles(points):
        return 2 * np.pi * ((freq @ points.T) % SPAN) / SPAN

    pixels = np.stack([np.repeat(np.arange(MAP), MAP), np.tile(np.arange(MAP), MAP)], axis=1)
    theta = angles(pixels)
    forward = np.zeros((4, FROWS, WIN))
    for m in range(4):
        at = PIX * m - WIN_AT[m]
        forward[m, :count, at : at + PIX] = np.cos(theta)
        forward[m, NFREQ : NFREQ + count, at : at + PIX] = -np.sin(theta)
    inverse = np.zeros((PIX, FROWS))
    inverse[:, :count] = twice * np.cos(theta).T
    inverse[:, NFREQ : NFREQ + count] = -twice * np.sin(theta).T
    taps = tap_offsets()
    phi = angles(taps)
    from_taps = np.zeros((FROWS, NTAPS))
    from_taps[:count, : len(taps)] = np.cos(phi)
    from_taps[NFREQ : NFREQ + count, : len(taps)] = np.sin(phi)
    to_taps = np.zeros((NTAPS, FROWS))
    to_taps[: len(taps), :count] = twice * np.cos(phi).T
    to_taps[: len(taps), NFREQ : NFREQ + count] = twice * np.sin(phi).T
    as_bf16 = lambda x: x.astype(np.float32).astype(jnp.bfloat16)
    return as_bf16(forward), as_bf16(inverse), bf16_pair(from_taps), bf16_pair(to_taps)


def dot(a, b):
    return jnp.dot(a, b, preferred_element_type=jnp.float32)


def dot_t(a, b):
    return lax.dot_general(a, b, (((1,), (1,)), ((), ())), preferred_element_type=jnp.float32)


def as_float(x):
    return x.astype(jnp.float32)


def as_row(ref):
    return ref[...].reshape(1, -1)


def fold8(x):
    return jnp.sum(x.reshape(-1, 8, x.shape[-1]), axis=0)


def pair_window(ref, m):
    return jnp.concatenate(
        [ref[g * GROUP + WIN_AT[m] : g * GROUP + WIN_AT[m] + WIN, :] for g in range(2)],
        axis=1,
    )


def put_pair(ref, m, pair):
    for g in range(2):
        at = g * GROUP + PIX * m
        ref[at : at + PIX, :] = pair[:, g * D : (g + 1) * D]


def whole(a):
    return pl.BlockSpec(a.shape, lambda i, n=len(a.shape): (0,) * n)


def start_all(copies):
    for copy in copies:
        copy.start()


def wait_all(copies):
    for copy in copies:
        copy.wait()


def conv_kernel(
    image_ref, tall_ref, wide_ref, small_ref, tall_mask_ref, wide_mask_ref, small_mask_ref,
    forward_ref, inverse_ref, from_taps_ref,
    conv_ref, khat_ref, moments_ref,
    product_ref, taps_ref, sums_ref,
):
    step = pl.program_id(0)

    @pl.when(step == 0)
    def _():
        sums_ref[...] = jnp.zeros_like(sums_ref)
        taps_ref[...] = jnp.zeros_like(taps_ref)
        for b in range(5):
            column = tall_ref[b, LONG_LO : LONG_LO + SPAN] * as_float(tall_mask_ref[b, LONG_LO : LONG_LO + SPAN])
            middle = column[MAP - 3 : MAP + 2] + wide_ref[:, 23 + b, :] * as_float(wide_mask_ref[:, 23 + b, :])
            middle = middle + small_ref[:, b, :] * as_float(small_mask_ref[:, b, :])
            taps_ref[SPAN * b : SPAN * b + SPAN, :] = column
            taps_ref[SPAN * b + MAP - 3 : SPAN * b + MAP + 2, :] = middle
        for r in range(5):
            at = 5 * SPAN + 2 * SIDE * r
            for lo in (LONG_LO, 28):
                row = wide_ref[r, lo : lo + SIDE] * as_float(wide_mask_ref[r, lo : lo + SIDE])
                taps_ref[at : at + SIDE, :] = row
                at += SIDE
        taps = taps_ref[...].astype(jnp.bfloat16)
        khat = dot(from_taps_ref[0], taps) + dot(from_taps_ref[1], taps)
        khat_ref[...] = khat * np.float32(1.0 / (SPAN * SPAN))

    for k in range(2):
        images = (2 * k, 2 * k + 1)
        spectra = [dot(forward_ref[m], pair_window(image_ref, m)) for m in images]
        for r in range(0, NFREQ, FREQ_ROWS):
            re, im = slice(r, r + FREQ_ROWS), slice(NFREQ + r, NFREQ + r + FREQ_ROWS)
            real, imag = khat_ref[re, :], khat_ref[im, :]
            for m, xhat in zip(images, spectra):
                for g in range(2):
                    cols = slice(g * D, (g + 1) * D)
                    xr, xi = xhat[re, cols], xhat[im, cols]
                    product_ref[m, re, cols] = (real * xr - imag * xi).astype(jnp.bfloat16)
                    product_ref[m, im, cols] = (real * xi + imag * xr).astype(jnp.bfloat16)
        for m in images:
            put_pair(conv_ref, m, dot(inverse_ref[...], product_ref[m]))
    conv = conv_ref[...]
    sums_ref[:8, :] += fold8(conv)
    sums_ref[8:, :] += fold8(conv * conv)

    @pl.when(step == pl.num_programs(0) - 1)
    def _():
        sums = [jnp.sum(sums_ref[8 * i : 8 * i + 8, :], axis=0, keepdims=True) for i in range(2)]
        put_everywhere(moments_ref, jnp.concatenate(sums, axis=0))


def conv_forward(image_rows, weights, masks, tables):
    rows = image_rows.shape[0]
    steps = rows // STEP
    forward, inverse, from_taps, _ = tables
    khat = jax.ShapeDtypeStruct((FROWS, D), jnp.float32)
    devices = lax.axis_size("dp") * lax.axis_size("mp")
    moments = jax.ShapeDtypeStruct((devices, 2, D), jnp.float32)
    return pl.pallas_call(
        conv_kernel,
        grid=(steps,),
        in_specs=[pl.BlockSpec((STEP, D), lambda i: (i, 0))]
        + [whole(a) for a in (*weights, *masks, forward, inverse, from_taps)],
        out_specs=[
            pl.BlockSpec((STEP, D), lambda i: (i, 0)),
            whole(khat),
            whole(moments),
        ],
        out_shape=[
            jax.ShapeDtypeStruct((rows, D), jnp.float32),
            khat,
            moments,
        ],
        scratch_shapes=[
            pltpu.VMEM((4, FROWS, 2 * D), jnp.bfloat16),
            pltpu.VMEM((NTAPS, D), jnp.float32),
            pltpu.VMEM((16, D), jnp.float32),
        ],
        compiler_params=pltpu.CompilerParams(vmem_limit_bytes=VMEM_LIMIT),
        cost_estimate=pl.CostEstimate(
            flops=4 * rows * D * FROWS, bytes_accessed=rows * D * 10, transcendentals=0
        ),
        name="conv_forward",
    )(image_rows, *weights, *masks, forward, inverse, from_taps)


def put_everywhere(ref, rows):
    ref[...] = jnp.broadcast_to(rows[None], ref.shape)


def arrived(ref):
    return jnp.sum(ref[...], axis=0)


def exchange(x):
    return lax.all_to_all(x, ("dp", "mp"), split_axis=0, concat_axis=0)


def batch_norm_terms(moments_ref, total):
    moments = arrived(moments_ref)
    mean = moments[0:1, :] * np.float32(1.0 / total)
    variance = moments[1:2, :] * np.float32(1.0 / total) - mean * mean
    return mean, lax.rsqrt(variance + BN_EPS)


def split_refs(refs):
    return (*refs[:3], refs[3 : 3 + SET], refs[3 + SET : 3 + 2 * SET], *refs[3 + 2 * SET :])


def mlp_kernel(total, *refs):
    blocks = lax.axis_size("mp")
    conv_hbm, image_hbm, grad_hbm, moments_ref = refs[:4]
    vectors, refs = [as_row(ref) for ref in refs[4:11]], refs[11:]
    own, direct, other = refs[:2], refs[2 : 1 + blocks], refs[1 + blocks : 2 * blocks]
    out_hbm, dbn_hbm, gw_hbm, bn_sums_ref, vec_ref = refs[2 * blocks : 5 + 2 * blocks]
    (
        conv_all, image_all, grad_all, set_a, set_b, w1_ref, w2_ref, mixed_ref, dnormed_ref, g1_ref, g2_ref,
        gw_ref, sum_ref, tile_sems, weight_sems, gw_sems,
    ) = split_refs(refs[5 + 2 * blocks :])
    rows = conv_all.shape[0]
    tiles = rows // TILE
    hidden = blocks * D
    core, place = lax.axis_index("dp") % 2, lax.axis_index("mp")

    def rows_of_tile(t):
        return pl.ds(pl.multiple_of(t * TILE, TILE), TILE)

    def reads(t):
        at = rows_of_tile(t)
        pairs = [(conv_hbm, conv_all), (grad_hbm, grad_all), (image_hbm, image_all)]
        return [
            pltpu.make_async_copy(a.at[at], b.at[at], tile_sems.at[i, t]) for i, (a, b) in enumerate(pairs)
        ]

    def writes(t, buffers):
        at = rows_of_tile(t)
        pairs = [(buffers[3], out_hbm), (buffers[4], dbn_hbm)]
        return [
            pltpu.make_async_copy(a, b.at[at], tile_sems.at[3 + i, t]) for i, (a, b) in enumerate(pairs)
        ]

    start_all(reads(0))

    def weight_copies(first, second):
        copies = []
        for s in range(blocks):
            at = slice(s * D, (s + 1) * D)
            source = (own[0], own[1]) if s == 0 else (first[s - 1], second[s - 1])
            copies.append(pltpu.make_async_copy(source[0], w1_ref.at[:, at], weight_sems.at[0, s]))
            copies.append(pltpu.make_async_copy(source[1], w2_ref.at[at, :], weight_sems.at[1, s]))
        return copies

    @pl.when(core == 0)
    def _():
        start_all(weight_copies(direct, other))

    @pl.when(core != 0)
    def _():
        start_all(weight_copies(other, direct))

    for t in range(1, tiles):
        start_all(reads(t))

    mean, bn_inv = batch_norm_terms(moments_ref, total)
    bn_gain, bn_bias, ln_gain, ln_bias, fc2_bias, layer_scale, fc1_bias = vectors
    scale = bn_inv * bn_gain
    bias_of = [fc1_bias[:, i * D : (i + 1) * D] for i in range(blocks)]
    bias = jnp.concatenate(
        [sum(jnp.where((place ^ s) == i, bias_of[i], 0.0) for i in range(blocks)) for s in range(blocks)], axis=1
    )
    sum_ref[...] = jnp.zeros_like(sum_ref)
    g1_ref[...] = jnp.zeros_like(g1_ref)
    g2_ref[...] = jnp.zeros_like(g2_ref)
    ones_row = jnp.where(lax.broadcasted_iota(jnp.int32, (16, TILE), 0) == 0, 1.0, 0.0).astype(jnp.bfloat16)
    set_a[7][D:, :] = ones_row
    set_b[7][D:, :] = ones_row

    def wide(x):
        return jnp.broadcast_to(x, (x.shape[0], 128))

    def across(x):
        return jnp.concatenate([x] * (D // 128), axis=1)

    def fetch(t, buffers):
        wait_all(reads(t))
        at = rows_of_tile(t)
        for whole, buffer in zip((conv_all, grad_all, image_all), buffers):
            buffer[...] = whole[at, :]

    def normalize(buffers):
        conv_ref, grad_ref = buffers[:2]
        normed_ref, dproj_ref, normed_t_ref, dproj_t_ref, mu_ref, inv_ref = buffers[5:11]
        for r in range(0, TILE, NORM_ROWS):
            at = slice(r, r + NORM_ROWS)
            out = (conv_ref[at, :] - mean) * scale + bn_bias
            mu = jnp.mean(out, axis=1, keepdims=True)
            center = out - mu
            inv = lax.rsqrt(jnp.mean(center * center, axis=1, keepdims=True) + LN_EPS)
            mu_ref[at, :] = wide(mu)
            inv_ref[at, :] = wide(inv)
            normed_ref[at, :] = (center * inv * ln_gain + ln_bias).astype(jnp.bfloat16)
            grad = as_float(grad_ref[at, :])
            dproj_ref[at, :] = (grad * layer_scale).astype(jnp.bfloat16)
            sum_ref[40:48, :] += fold8(grad)
        normed_t_ref[:D, :] = jnp.transpose(normed_ref[...])
        dproj_t_ref[...] = jnp.transpose(dproj_ref[...])

    root = np.float32(np.sqrt(2.0 / np.pi))
    cubic = np.float32(0.044715 * np.sqrt(2.0 / np.pi))

    def gelu_chunk(c, buffers):
        normed_ref, dproj_ref, act_ref, dhid_ref = buffers[5], buffers[6], buffers[11], buffers[12]
        cols = slice(c * CHUNK, (c + 1) * CHUNK)
        hid_all = dot(normed_ref[...], w1_ref[:, cols])
        dact_all = dot_t(dproj_ref[...], w2_ref[cols, :])
        for r in range(0, TILE, GELU_ROWS):
            hid = hid_all[r : r + GELU_ROWS] + bias[:, cols]
            square = hid * hid
            th = jnp.tanh(hid * (root + cubic * square))
            half = 0.5 + 0.5 * th
            act = hid * half
            slope = half + act * (1.0 - th) * (root + 3 * cubic * square)
            act_ref[r : r + GELU_ROWS, cols] = act.astype(jnp.bfloat16)
            dhid_ref[r : r + GELU_ROWS, cols] = (dact_all[r : r + GELU_ROWS] * slope).astype(jnp.bfloat16)

    def finish_rows(r, buffers):
        conv_ref, grad_ref, image_ref, out_ref, dbn_ref = buffers[:5]
        mu_ref, inv_ref = buffers[9:11]
        at = slice(r, r + LAST_ROWS)
        mixed = mixed_ref[at, :] + fc2_bias
        dnormed = dnormed_ref[at, :]
        out_ref[at, :] = (as_float(image_ref[at, :]) + layer_scale * mixed).astype(jnp.bfloat16)
        conv = conv_ref[at, :] - mean
        bn_hat = conv * bn_inv
        inv = across(inv_ref[at, :])
        ln_hat = (conv * scale + bn_bias - across(mu_ref[at, :])) * inv
        d_hat = dnormed * ln_gain
        first = jnp.mean(d_hat, axis=1, keepdims=True)
        second = jnp.mean(d_hat * ln_hat, axis=1, keepdims=True)
        dbn = inv * (d_hat - first - ln_hat * second)
        dbn_ref[at, :] = dbn
        sum_ref[0:8, :] += fold8(dbn * bn_hat)
        sum_ref[8:16, :] += fold8(dbn)
        sum_ref[16:24, :] += fold8(dnormed * ln_hat)
        sum_ref[24:32, :] += fold8(dnormed)
        sum_ref[32:40, :] += fold8(as_float(grad_ref[at, :]) * mixed)

    chunks = hidden // CHUNK
    parts = TILE // LAST_ROWS

    def step(ahead, now):
        if now is not None:
            act_ref, dhid_ref = now[11:13]
            mixed_ref[...] = dot(act_ref[...], w2_ref[...])
            dnormed_ref[...] = dot_t(dhid_ref[...], w1_ref[...])
        if ahead is not None:
            normalize(ahead)
        for c in range(chunks):
            if ahead is not None:
                gelu_chunk(c, ahead)
            if now is not None:
                cols = slice(c * CHUNK, (c + 1) * CHUNK)
                g1_ref[:, cols] += dot(now[7][...], dhid_ref[:, cols])
                g2_ref[:, cols] += dot(now[8][...], act_ref[:, cols])
                for i in range(c * parts // chunks, (c + 1) * parts // chunks):
                    finish_rows(i * LAST_ROWS, now)

    def two_steps(i, _):
        fetch(2 * i + 1, set_b)

        @pl.when(i > 0)
        def _():
            wait_all(writes(2 * i - 2, set_a))

        step(set_b, set_a)
        start_all(writes(2 * i, set_a))
        fetch(2 * i + 2, set_a)

        @pl.when(i > 0)
        def _():
            wait_all(writes(2 * i - 1, set_b))

        step(set_a, set_b)
        start_all(writes(2 * i + 1, set_b))
        return 0

    fetch(0, set_a)
    wait_all(weight_copies(direct, other))
    step(set_a, None)
    lax.fori_loop(0, (tiles - 1) // 2, two_steps, 0)
    last = tiles - 1
    if tiles % 2 == 0:
        fetch(last, set_b)
        if tiles > 2:
            wait_all(writes(last - 3, set_a))
        step(set_b, set_a)
        start_all(writes(last - 1, set_a))
        if tiles > 2:
            wait_all(writes(last - 2, set_b))
        step(None, set_b)
        start_all(writes(last, set_b))
    else:
        if tiles > 1:
            wait_all(writes(last - 2, set_a))
        step(None, set_a)
        start_all(writes(last, set_a))

    chips, size = gw_ref.shape[1] // 2, gw_ref.shape[2]
    ring = plane_ring(2 * chips)
    gw_copy = lambda s: pltpu.make_async_copy(gw_ref.at[s], gw_hbm.at[:, s], gw_sems.at[s])
    for s in range(blocks):
        cols = slice(s * D, (s + 1) * D)
        vec_ref[pl.ds(4 + (place ^ s), 1), :] = g1_ref[D : D + 1, cols]
        for i in range(chips):
            rows_of = slice(i * size, (i + 1) * size)
            gw_ref[s, ring.index(2 * i)] = g1_ref[rows_of, cols].astype(jnp.bfloat16)
            gw_ref[s, ring.index(2 * i + 1)] = g2_ref[rows_of, cols].astype(jnp.bfloat16)
        gw_copy(s).start()

    sums = [jnp.sum(sum_ref[8 * i : 8 * i + 8, :], axis=0, keepdims=True) for i in range(6)]
    put_everywhere(bn_sums_ref, jnp.concatenate(sums[:2], axis=0))
    vec_ref[0:4, :] = jnp.concatenate(sums[2:5] + [sums[5] * layer_scale], axis=0)
    for s in range(blocks):
        gw_copy(s).wait()
    first_set, second_set = (set_a, set_b) if tiles % 2 == 1 else (set_b, set_a)
    if tiles > 1:
        wait_all(writes(last - 1, second_set))
    wait_all(writes(last, first_set))


def mlp(total, conv, image_rows, out_grad, moments, vectors, own, direct, other):
    rows = conv.shape[0]
    tiles = rows // TILE
    blocks, chips = lax.axis_size("mp"), lax.axis_size("dp") // 2
    hidden = blocks * D
    vmem, hbm = pl.BlockSpec(memory_space=pltpu.VMEM), pl.BlockSpec(memory_space=pl.ANY)
    f32, bf16 = jnp.float32, jnp.bfloat16
    return pl.pallas_call(
        lambda *refs: mlp_kernel(total, *refs),
        in_specs=[hbm] * 3 + [vmem] * 8 + [hbm] * (2 * blocks),
        out_specs=[hbm] * 3 + [vmem] * 2,
        out_shape=[
            jax.ShapeDtypeStruct((rows, D), bf16),
            jax.ShapeDtypeStruct((rows, D), f32),
            jax.ShapeDtypeStruct((2 * chips, blocks, D // chips, D), bf16),
            jax.ShapeDtypeStruct((2 * chips * blocks, 2, D), f32),
            jax.ShapeDtypeStruct((4 + blocks, D), f32),
        ],
        scratch_shapes=[
            pltpu.VMEM((rows, D), f32),
            pltpu.VMEM((rows, D), bf16),
            pltpu.VMEM((rows, D), bf16),
        ]
        + [
            pltpu.VMEM((TILE, D), f32),
            pltpu.VMEM((TILE, D), bf16),
            pltpu.VMEM((TILE, D), bf16),
            pltpu.VMEM((TILE, D), bf16),
            pltpu.VMEM((TILE, D), f32),
            pltpu.VMEM((TILE, D), bf16),
            pltpu.VMEM((TILE, D), bf16),
            pltpu.VMEM((D + 16, TILE), bf16),
            pltpu.VMEM((D, TILE), bf16),
            pltpu.VMEM((TILE, 128), f32),
            pltpu.VMEM((TILE, 128), f32),
            pltpu.VMEM((TILE, hidden), bf16),
            pltpu.VMEM((TILE, hidden), bf16),
        ]
        * 2
        + [pltpu.VMEM((D, hidden), bf16), pltpu.VMEM((hidden, D), bf16)]
        + [pltpu.VMEM((TILE, D), f32)] * 2
        + [
            pltpu.VMEM((D + 16, hidden), f32),
            pltpu.VMEM((D, hidden), f32),
            pltpu.VMEM((blocks, 2 * chips, D // chips, D), bf16),
            pltpu.VMEM((48, D), f32),
            pltpu.SemaphoreType.DMA((5, tiles)),
            pltpu.SemaphoreType.DMA((2, blocks)),
            pltpu.SemaphoreType.DMA((blocks,)),
        ],
        compiler_params=pltpu.CompilerParams(vmem_limit_bytes=VMEM_LIMIT),
        cost_estimate=pl.CostEstimate(
            flops=12 * rows * D * hidden, bytes_accessed=rows * D * 20, transcendentals=rows * hidden
        ),
        name="mlp",
    )(conv, image_rows, out_grad, moments, *vectors, *own, *direct, *other)


def spectra_kernel(
    total, dbn_ref, conv_ref, image_ref, khat_ref, moments_ref, bn_sums_ref, vec_ref, bn_gain_ref,
    forward_ref, to_taps_ref,
    product_hbm, taps_ref,
    product_ref, dconv_ref, dhat_ref, all_taps_ref, sems,
):
    step = pl.program_id(0)

    def writes(at, images):
        return [pltpu.make_async_copy(product_ref.at[m], product_hbm.at[4 * at + m], sems.at[m]) for m in images]

    @pl.when(step > 0)
    def _():
        wait_all(writes(step - 1, range(4)))

    mean, bn_inv = batch_norm_terms(moments_ref, total)
    bn_sums = arrived(bn_sums_ref) * np.float32(1.0 / total)
    gain = as_row(bn_gain_ref) * bn_inv
    slope, shift = bn_sums[0:1, :], bn_sums[1:2, :]

    @pl.when(step == 0)
    def _():
        dhat_ref[...] = jnp.zeros_like(dhat_ref)

    for r in range(0, STEP, LAST_ROWS):
        at = slice(r, r + LAST_ROWS)
        bn_hat = (conv_ref[at, :] - mean) * bn_inv
        dconv = gain * (dbn_ref[at, :] - shift - bn_hat * slope)
        dconv_ref[at, :] = dconv.astype(jnp.bfloat16)
    for k in range(2):
        images = (2 * k, 2 * k + 1)
        spectra = [dot(forward_ref[m], pair_window(dconv_ref, m)) for m in images]
        image_spectra = [dot(forward_ref[m], pair_window(image_ref, m)) for m in images]
        for r in range(0, NFREQ, FREQ_ROWS):
            re, im = slice(r, r + FREQ_ROWS), slice(NFREQ + r, NFREQ + r + FREQ_ROWS)
            real, imag = khat_ref[re, :], khat_ref[im, :]
            tap_re, tap_im = [], []
            for m, ghat, xhat in zip(images, spectra, image_spectra):
                for g in range(2):
                    cols = slice(g * D, (g + 1) * D)
                    gr, gi = ghat[re, cols], ghat[im, cols]
                    product_ref[m, re, cols] = (real * gr + imag * gi).astype(jnp.bfloat16)
                    product_ref[m, im, cols] = (real * gi - imag * gr).astype(jnp.bfloat16)
                    xr, xi = xhat[re, cols], xhat[im, cols]
                    tap_re.append(xr * gr + xi * gi)
                    tap_im.append(xr * gi - xi * gr)
            dhat_ref[re, :] += tree_sum(tap_re)
            dhat_ref[im, :] += tree_sum(tap_im)
        start_all(writes(step, images))

    @pl.when(step == pl.num_programs(0) - 1)
    def _():
        dhat = dhat_ref[...]
        high = dhat.astype(jnp.bfloat16)
        low = (dhat - as_float(high)).astype(jnp.bfloat16)
        taps = dot(to_taps_ref[0], high) + dot(to_taps_ref[0], low) + dot(to_taps_ref[1], high)
        all_taps_ref[...] = taps * np.float32(1.0 / (SPAN * SPAN))
        all_taps_ref[REST : REST + vec_ref.shape[0], :] = vec_ref[...]
        devices, size, _ = taps_ref.shape
        for i in range(devices):
            if i * size < NTAPS:
                taps_ref[i] = all_taps_ref[i * size : (i + 1) * size, :].astype(jnp.bfloat16)
            else:
                taps_ref[i] = jnp.zeros((size, D), jnp.bfloat16)
        wait_all(writes(step, range(4)))


def gradient_spectra(total, dbn, conv, image_rows, khat, moments, bn_sums, vec, bn_gain, tables):
    rows = conv.shape[0]
    steps = rows // STEP
    forward, _, _, to_taps = tables
    devices = lax.axis_size("dp") * lax.axis_size("mp")
    f32, bf16 = jnp.float32, jnp.bfloat16
    block = pl.BlockSpec((STEP, D), lambda i: (i, 0))
    taps = jax.ShapeDtypeStruct((devices, max(8, NTAPS // devices), D), bf16)
    return pl.pallas_call(
        lambda *refs: spectra_kernel(total, *refs),
        grid=(steps,),
        in_specs=[block] * 3
        + [whole(a) for a in (khat, moments, bn_sums, vec, bn_gain, forward, to_taps)],
        out_specs=[pl.BlockSpec(memory_space=pl.ANY), whole(taps)],
        out_shape=[jax.ShapeDtypeStruct((4 * steps, FROWS, 2 * D), bf16), taps],
        scratch_shapes=[
            pltpu.VMEM((4, FROWS, 2 * D), bf16),
            pltpu.VMEM((STEP, D), bf16),
            pltpu.VMEM((FROWS, D), f32),
            pltpu.VMEM((NTAPS, D), f32),
            pltpu.SemaphoreType.DMA((4,)),
        ],
        compiler_params=pltpu.CompilerParams(vmem_limit_bytes=VMEM_LIMIT),
        cost_estimate=pl.CostEstimate(
            flops=2 * rows * D * FROWS, bytes_accessed=rows * D * 26, transcendentals=0
        ),
        name="gradient_spectra",
    )(dbn, conv, image_rows, khat, moments, bn_sums, vec, bn_gain, forward, to_taps)


def inverse_kernel(product_ref, grad_ref, inverse_ref, in_grad_ref, image_grad_ref):
    for m in range(4):
        put_pair(image_grad_ref, m, dot(inverse_ref[...], product_ref[m]))
    in_grad_ref[...] = (image_grad_ref[...] + as_float(grad_ref[...])).astype(jnp.bfloat16)


def image_gradient(product, out_grad, tables):
    rows = out_grad.shape[0]
    inverse = tables[1]
    block = pl.BlockSpec((STEP, D), lambda i: (i, 0))
    return pl.pallas_call(
        inverse_kernel,
        grid=(rows // STEP,),
        in_specs=[pl.BlockSpec((4, FROWS, 2 * D), lambda i: (i, 0, 0)), block, whole(inverse)],
        out_specs=block,
        out_shape=jax.ShapeDtypeStruct((rows, D), jnp.bfloat16),
        scratch_shapes=[pltpu.VMEM((STEP, D), jnp.float32)],
        compiler_params=pltpu.CompilerParams(vmem_limit_bytes=VMEM_LIMIT),
        cost_estimate=pl.CostEstimate(
            flops=2 * rows * D * FROWS, bytes_accessed=rows * D * 10, transcendentals=0
        ),
        name="image_gradient",
    )(product, out_grad, inverse)


def finish_kernel(chips, *refs):
    mine, other = refs[:chips], refs[chips : 2 * chips]
    tall_mask_ref, wide_mask_ref, small_mask_ref, bn_sums_ref = refs[2 * chips : 2 * chips + 4]
    tall_ref, wide_ref, small_ref, fc1_ref, fc2_ref = refs[2 * chips + 4 : 2 * chips + 9]
    vector_refs, taps_ref, fc2_t_ref = refs[2 * chips + 9 : -2], refs[-2], refs[-1]
    core, chip = lax.axis_index("dp") % 2, lax.axis_index("dp") // 2
    places, place = lax.axis_size("mp"), lax.axis_index("mp")
    size, count = taps_ref.shape[0] // (2 * chips * places), D // chips
    for k in range(chips):
        at = pl.ds(pl.multiple_of((chip ^ k) * count, 8), count)
        mine_rows, other_rows = as_float(mine[k][...]), as_float(other[k][...])
        for s in range(places):
            for owner, rows in ((core, mine_rows), (1 - core, other_rows)):
                device = (2 * (chip ^ k) + owner) * places + (place ^ s)
                taps_ref[pl.ds(pl.multiple_of(device * size, 8), size), :] = rows[s * size : (s + 1) * size]

        @pl.when(core == 0)
        def _():
            fc1_ref[at, :] = mine_rows[places * size :]
            fc2_t_ref[at, :] = other_rows[places * size :]

        @pl.when(core != 0)
        def _():
            fc1_ref[at, :] = other_rows[places * size :]
            fc2_t_ref[at, :] = mine_rows[places * size :]

    fc2_ref[...] = jnp.transpose(fc2_t_ref[...])
    bn_sums = arrived(bn_sums_ref)
    rows = [bn_sums[0:1], bn_sums[1:2]] + [taps_ref[REST + i : REST + i + 1, :] for i in range(4)]
    rows.append(taps_ref[pl.ds(REST + 4 + place, 1), :])
    for ref, row in zip(vector_refs, rows):
        ref[...] = row.reshape(ref.shape)
    tall_ref[...] = jnp.zeros_like(tall_ref)
    wide_ref[...] = jnp.zeros_like(wide_ref)
    for b in range(5):
        column = taps_ref[SPAN * b : SPAN * b + SPAN, :]
        middle = column[MAP - 3 : MAP + 2, :]
        tall_ref[b, LONG_LO : LONG_LO + SPAN] = column * as_float(tall_mask_ref[b, LONG_LO : LONG_LO + SPAN])
        small_ref[:, b, :] = middle * as_float(small_mask_ref[:, b, :])
        wide_ref[:, 23 + b, :] = middle * as_float(wide_mask_ref[:, 23 + b, :])
    for r in range(5):
        at = 5 * SPAN + 2 * SIDE * r
        for lo in (LONG_LO, 28):
            wide_ref[r, lo : lo + SIDE] = taps_ref[at : at + SIDE, :] * as_float(wide_mask_ref[r, lo : lo + SIDE])
            at += SIDE


def finish(mine, other, masks, bn_sums):
    chips, places = len(mine), lax.axis_size("mp")
    size = (mine[0].shape[0] - D // chips) // places
    vmem = pl.BlockSpec(memory_space=pltpu.VMEM)
    square = jax.ShapeDtypeStruct((D, D), jnp.float32)
    return pl.pallas_call(
        lambda *refs: finish_kernel(chips, *refs),
        in_specs=[vmem] * (2 * chips + 4),
        out_specs=[vmem] * 12,
        out_shape=[jax.ShapeDtypeStruct(m.shape, jnp.float32) for m in masks] + [square, square]
        + [jax.ShapeDtypeStruct((D,), jnp.float32)] * 7,
        scratch_shapes=[pltpu.VMEM((2 * chips * places * size, D), jnp.float32), pltpu.VMEM((D, D), jnp.float32)],
        compiler_params=pltpu.CompilerParams(vmem_limit_bytes=FINISH_VMEM),
        name="finish",
    )(*mine, *other, *masks, bn_sums)


def swap(x, axis, bit):
    size = lax.axis_size(axis)
    return lax.ppermute(x, axis, [(i, i ^ bit) for i in range(size)])


def swap_places(parts):
    got = [swap(x, "mp", s + 1) for s, x in reversed(list(enumerate(parts)))]
    return got[::-1]


def tree_sum(terms):
    while len(terms) > 1:
        terms = [a + b for a, b in zip(terms[::2], terms[1::2])]
    return terms[0]


def plane_steps():
    return range(2, lax.axis_size("dp"), 2)


def first_weights(fc1_weight, fc2_weight):
    mine = jnp.where(lax.axis_index("dp") % 2 == 0, fc1_weight, fc2_weight)
    powers = [1 << i for i in range(lax.axis_size("mp").bit_length() - 1)]
    return {s: swap(mine, "mp", s) for s in reversed(powers)}


def other_weights(got):
    for s in range(1, lax.axis_size("mp")):
        if s not in got:
            high = 1 << (s.bit_length() - 1)
            got[s] = swap(got[high], "mp", s ^ high)
    return [got[s] for s in range(1, lax.axis_size("mp"))]


def plane_ring(size):
    return [0, 1, 3, 2, 6, 7, 5, 4] if size == 8 else list(range(size))


def reduce_weight_grads(parts):
    groups = [plane_ring(lax.axis_size("dp"))]
    mine = lax.psum_scatter(parts, "dp", scatter_dimension=0, axis_index_groups=groups, tiled=False)
    return lax.optimization_barrier(mine)


def message_kernel(taps_ref, weights_ref, own_ref, *message_refs):
    taps = jnp.sum(as_float(taps_ref[...]), axis=0)
    own_ref[...] = jnp.concatenate([taps, as_float(weights_ref[0])], axis=0)
    for s, ref in enumerate(message_refs):
        ref[...] = jnp.concatenate([taps, as_float(weights_ref[s + 1])], axis=0).astype(jnp.bfloat16)


def total_kernel(own_ref, *refs):
    got, total_ref = refs[:-1], refs[-1]
    size = (total_ref.shape[0] - own_ref.shape[0]) // len(got)
    rows = [own_ref[...]] + [as_float(ref[...]) for ref in got]
    weights = tree_sum([x[size:] for x in rows])
    total_ref[...] = jnp.concatenate([x[:size] for x in rows] + [weights], axis=0).astype(jnp.bfloat16)


def reduce_rest(taps, weights):
    places, size, count = lax.axis_size("mp"), taps.shape[1], weights.shape[1]
    vmem = pl.BlockSpec(memory_space=pltpu.VMEM)
    rows = lambda n, kind: jax.ShapeDtypeStruct((n, D), kind)
    own, *messages = pl.pallas_call(
        message_kernel,
        in_specs=[vmem] * 2,
        out_specs=[vmem] * places,
        out_shape=[rows(size + count, jnp.float32)] + [rows(size + count, jnp.bfloat16)] * (places - 1),
        compiler_params=pltpu.CompilerParams(vmem_limit_bytes=SMALL_VMEM),
        name="messages",
    )(taps, weights)
    got = swap_places(messages)
    mine = pl.pallas_call(
        total_kernel,
        in_specs=[vmem] * places,
        out_specs=vmem,
        out_shape=rows(places * size + count, jnp.bfloat16),
        compiler_params=pltpu.CompilerParams(vmem_limit_bytes=SMALL_VMEM),
        name="totals",
    )(own, *got)
    mine = [mine] + [swap(mine, "dp", s) for s in plane_steps()]
    return mine, [swap(x, "dp", 1) for x in mine]


def on_device(
    image_rows, tall_weight, wide_weight, small_weight, tall_mask, wide_mask, small_mask,
    bn_gain, bn_bias, ln_gain, ln_bias, fc1_weight, fc1_bias, fc2_weight, fc2_bias, layer_scale, out_grad,
):
    rows = image_rows.shape[0]
    total = rows * lax.axis_size("dp") * lax.axis_size("mp")
    tables = tuple(jnp.asarray(t) for t in transform_tables())
    turn = lambda x: jnp.swapaxes(x, 0, 1)
    masks = (turn(tall_mask), wide_mask, small_mask)
    first = first_weights(fc1_weight, fc2_weight)

    conv, khat, moments = conv_forward(
        image_rows, (turn(tall_weight), wide_weight, small_weight), masks, tables
    )
    khat, first = lax.optimization_barrier((khat, first))
    early = {s: swap(x, "dp", 1) for s, x in first.items()}
    moments, direct, early = lax.optimization_barrier((exchange(moments), other_weights(first), early))
    other = [early[s + 1] if s + 1 in early else swap(x, "dp", 1) for s, x in enumerate(direct)]
    block_out, dbn, gw, bn_sums, vec = mlp(
        total, conv, image_rows, out_grad, moments,
        (bn_gain, bn_bias, ln_gain, ln_bias, fc2_bias, layer_scale, fc1_bias),
        (fc1_weight, fc2_weight), direct, other,
    )
    bn_sums = exchange(bn_sums)
    weights = reduce_weight_grads(gw)
    product, taps = gradient_spectra(total, dbn, conv, image_rows, khat, moments, bn_sums, vec, bn_gain, tables)
    in_grad = image_gradient(product, out_grad, tables)
    taps, in_grad = lax.optimization_barrier((exchange(taps), in_grad))
    mine, other = reduce_rest(taps, weights)
    tall_grad, wide_grad, small_grad, fc1_grad, fc2_grad, *vec = finish(mine, other, masks, bn_sums)
    tall_grad = turn(tall_grad)
    return (
        block_out, in_grad, tall_grad, wide_grad, small_grad, vec[0], vec[1], vec[2], vec[3],
        fc1_grad, vec[6], fc2_grad, vec[5], vec[4],
    )


def solution(mesh):
    rows, none = P(("dp", "mp"), None), P()
    return jax.shard_map(
        on_device,
        mesh=mesh,
        in_specs=(rows,) + (none,) * 10 + (P(None, "mp"), none, P("mp", None), none, none, rows),
        out_specs=(rows, rows) + (none,) * 7 + (P(None, "mp"), P("mp"), P("mp", None), none, none),
        check_vma=False,
    )
```
